32 devices in a mesh: gz: 2 (over core), row: 4 (over y, x), col: 4 (over z).
Axes of the slice: x: 2, y: 2, z: 4, core: 2. Of those that a mesh axis runs over, the one named last changes fastest.
Arguments:
- ancestor: float32 [4096, 2048], P('row', 'col'), may hold values from -6 to 6
- lower_panel: bfloat16 [2, 8, 24, 128, 128], P('gz', 'col', 'row'), may hold values from -6 to 6
- row_ids: int32 [2, 8, 24], P('gz', 'col', 'row'), may hold values from 0 to 7, as said below
- row_counts: int32 [2, 8, 4], P('gz', 'col', 'row'), may hold values from 1 to 6
- diag_inverse: bfloat16 [2, 8, 128, 128], P('gz', 'col'), may hold values from -0.5 to 0.5
- upper_panel: bfloat16 [2, 8, 12, 128, 128], P('gz', 'row', 'col'), may hold values from -0.1875 to 0.1875
- col_ids: int32 [2, 8, 12], P('gz', 'row', 'col'), may hold values from 0 to 3, as said below
- col_counts: int32 [2, 8, 4], P('gz', 'row', 'col'), may hold values from 1 to 3
Outputs:
- updated: float32 [4096, 2048], P('row', 'col')
The draws below stay inside these ranges and needn't reach their ends.
Inputs may be any that keep to these rules, and one draw needn't show every extreme that they name: `row_ids`: within each layer, supernode and process row the 6 slots name distinct local block rows. `col_ids`: within each layer, supernode and process column the 3 slots name distinct local block columns.
All inputs are finite; a program needn't handle non-finite values.
Results may differ from the reference program's by a relative error of at most 0.0026.
Values may be sent and summed in bfloat16 or wider, within the bound.
No kernel may reach another device: no remote copies, remote signals or barrier semaphores. Data moves between devices by JAX's collectives and lax.ppermute only.
A program may use at most 128 MiB of HBM per device.

```python
import jax
import jax.numpy as jnp
from jax import lax

B = 128
NAR_DEV = 8
NAC_DEV = 4
RL = 6
CL = 3
LAYERS = 2
KS = 8
RSLOTS = 24
CSLOTS = 12
NAR = 32
NAC = 16


def pick_subsets(key, leading, slots, pool):
    scores = jax.random.randint(key, leading + (pool,), 0, 1 << 20) * pool + jnp.arange(pool, dtype=jnp.int32)
    ranking = jnp.argsort(scores, axis=-1)
    return ranking[..., :slots].astype(jnp.int32)


def counts_reaching(key, shape, most):
    counts = jax.random.randint(jax.random.fold_in(key, 1), shape, 1, most + 1)
    flat = counts.reshape(-1)
    position = jax.random.randint(jax.random.fold_in(key, 2), (), 0, flat.shape[0])
    flat = flat.at[position].set(most)
    return flat.reshape(shape).astype(jnp.int32)


def draw_row_ids(key, part):
    groups = RSLOTS // RL
    chosen = pick_subsets(jax.random.fold_in(key, 11), (LAYERS, KS, groups), RL, NAR_DEV)
    return chosen.reshape(LAYERS, KS, RSLOTS)


def draw_row_counts(key, part):
    groups = RSLOTS // RL
    return counts_reaching(jax.random.fold_in(key, 12), (LAYERS, KS, groups), RL)


def draw_col_ids(key, part):
    groups = CSLOTS // CL
    chosen = pick_subsets(jax.random.fold_in(key, 21), (LAYERS, KS, groups), CL, NAC_DEV)
    return chosen.reshape(LAYERS, KS, CSLOTS)


def draw_col_counts(key, part):
    groups = CSLOTS // CL
    return counts_reaching(jax.random.fold_in(key, 22), (LAYERS, KS, groups), CL)


def levels(own_key, dims, cuts, least, top_value):
    factor_of = 1.0
    for axis_at, blocks in cuts:
        draws = jax.random.uniform(jax.random.fold_in(jax.random.fold_in(own_key, 6), axis_at), (blocks,), jnp.float32, least / len(cuts), top_value / len(cuts))
        factor_of = factor_of * jnp.repeat(jnp.exp(draws), dims[axis_at] // blocks).reshape((-1,) + (1,) * (len(dims) - 1 - axis_at))
    return factor_of


def normal_values(stream_key, dims, deviation, bound, pieces=(), held_as=jnp.bfloat16):
    array = deviation * jax.random.normal(stream_key, dims, jnp.float32)
    if pieces:
        array = array * levels(stream_key, dims, pieces, -0.22, 0.18)
    return jnp.clip(array, -bound, bound).astype(held_as)


def setup_inputs(seed: int = 0) -> dict:
    key_list = jax.random.split(jax.random.key(seed), 9)
    ancestor = normal_values(key_list[0], (NAR * B, NAC * B), 1.0, 6.0, ((0, 4), (1, 4)), jnp.float32)
    lower_panel = normal_values(key_list[1], (LAYERS, KS, RSLOTS, B, B), 1.0, 6.0, ((0, 2), (1, 4), (2, 4)))
    row_ids = draw_row_ids(jax.random.fold_in(key_list[8], 71), 0)
    row_counts = draw_row_counts(jax.random.fold_in(key_list[8], 71), 0)
    diag_inverse = normal_values(key_list[4], (LAYERS, KS, B, B), B ** -0.5, 0.5, ((0, 2), (1, 4)))
    upper_panel = normal_values(key_list[5], (LAYERS, KS, CSLOTS, B, B), (8 * B) ** -0.5, 0.1875, ((0, 2), (1, 4), (2, 4)))
    col_ids = draw_col_ids(jax.random.fold_in(key_list[8], 71), 0)
    col_counts = draw_col_counts(jax.random.fold_in(key_list[8], 71), 0)
    return dict(ancestor=ancestor, lower_panel=lower_panel, row_ids=row_ids, row_counts=row_counts, diag_inverse=diag_inverse, upper_panel=upper_panel, col_ids=col_ids, col_counts=col_counts)


def reference(ancestor, lower_panel, row_ids, row_counts, diag_inverse, upper_panel, col_ids, col_counts):
    highest = lax.Precision.HIGHEST
    slot_rows = jnp.arange(RSLOTS, dtype=jnp.int32)
    group_rows = slot_rows // RL
    slot_cols = jnp.arange(CSLOTS, dtype=jnp.int32)
    group_cols = slot_cols // CL
    updates = jnp.zeros((NAR, B, NAC, B), jnp.float32)
    for layer_index in range(LAYERS):
        def apply_one(accumulated, supernode_items):
            lower, rows, row_live, inverse, upper, cols, col_live = supernode_items
            solved = jnp.einsum('sab,bc->sac', lower.astype(jnp.float32), inverse.astype(jnp.float32), precision=highest)
            solved = lax.optimization_barrier(solved.astype(jnp.bfloat16)).astype(jnp.float32)
            alive_rows = (slot_rows % RL) < row_live[group_rows]
            solved = jnp.where(alive_rows[:, None, None], solved, jnp.float32(0.0))
            alive_cols = (slot_cols % CL) < col_live[group_cols]
            upper_live = jnp.where(alive_cols[:, None, None], upper.astype(jnp.float32), jnp.float32(0.0))
            tiles = jnp.einsum('sac,tcd->stad', solved, upper_live, precision=highest)
            global_rows = (group_rows * NAR_DEV + rows).astype(jnp.int32)
            global_cols = (group_cols * NAC_DEV + cols).astype(jnp.int32)
            accumulated = accumulated.at[global_rows[:, None], :, global_cols[None, :], :].add(tiles)
            return accumulated, None

        updates, _ = lax.scan(apply_one, updates, (lower_panel[layer_index], row_ids[layer_index], row_counts[layer_index], diag_inverse[layer_index], upper_panel[layer_index], col_ids[layer_index], col_counts[layer_index]))
    return ancestor - updates.reshape(NAR * B, NAC * B)
```

```python
import functools

import jax
import jax.numpy as jnp
from jax import lax
from jax.experimental import pallas as pl
from jax.experimental.pallas import tpu as pltpu
from jax.sharding import PartitionSpec as P

VMEM_LIMIT = 24 * 1024 * 1024
ID_ROWS = 16


def whole_vmem():
    return pl.BlockSpec(memory_space=pltpu.VMEM)


def whole_smem():
    return pl.BlockSpec(memory_space=pltpu.SMEM)


def prepare_kernel(row_ids, row_counts, col_ids, col_counts, lower, inverse, upper, both, first, second, spread):
    supernodes, slots, width, _ = lower.shape
    chunk = slots * width + ID_ROWS
    for k, half in enumerate((first, second)):
        tiles = lower[k].reshape(slots * width, width)
        solved = jnp.dot(tiles, inverse[k], preferred_element_type=jnp.float32).astype(jnp.bfloat16)
        half[0 : slots * width, :] = solved
        both[k * chunk : k * chunk + slots * width, :] = solved
        at_row = lax.broadcasted_iota(jnp.int32, (ID_ROWS, width), 0)
        ids = jnp.zeros((ID_ROWS, width), jnp.int32)
        for s in range(slots):
            place = jnp.where(s < row_counts[0, k, 0], row_ids[0, k, s] + 1, 0)
            ids = jnp.where(at_row == s, place, ids)
        ids = ids.astype(jnp.float32).astype(jnp.bfloat16)
        half[slots * width : chunk, :] = ids
        both[k * chunk + slots * width : (k + 1) * chunk, :] = ids
    spread[...] = jnp.zeros_like(spread)
    for k in range(supernodes):
        for c in range(upper.shape[1]):

            @pl.when(c < col_counts[0, k, 0])
            def _():
                at = pl.multiple_of(col_ids[0, k, c] * width, width)
                spread[k * width : (k + 1) * width, pl.ds(at, width)] = upper[k, c]


def prepare(lower, row_ids, row_counts, inverse, upper, col_ids, col_counts, col_blocks):
    supernodes, slots, width, _ = lower.shape
    chunk = slots * width + ID_ROWS
    return pl.pallas_call(
        prepare_kernel,
        out_shape=(
            jax.ShapeDtypeStruct((supernodes * chunk, width), jnp.bfloat16),
            jax.ShapeDtypeStruct((chunk, width), jnp.bfloat16),
            jax.ShapeDtypeStruct((chunk, width), jnp.bfloat16),
            jax.ShapeDtypeStruct((supernodes * width, col_blocks * width), jnp.bfloat16),
        ),
        in_specs=[whole_smem()] * 4 + [whole_vmem()] * 3,
        out_specs=(whole_vmem(),) * 4,
        compiler_params=pltpu.CompilerParams(vmem_limit_bytes=VMEM_LIMIT),
        name="solve_and_pack",
    )(row_ids, row_counts, col_ids, col_counts, lower, inverse, upper)


def accumulate_kernel(slots, col_axis, row_axis, items, payloads, base_count, *refs):
    panels = refs[:payloads]
    uppers = refs[payloads : payloads + 4]
    bases = refs[payloads + 4 : payloads + 4 + base_count]
    out = refs[payloads + 4 + base_count]
    left, right = refs[payloads + 5 + base_count :]
    width = panels[0].shape[1]
    chunk = slots * width + ID_ROWS
    step = pl.program_id(0)

    @pl.when(step == 0)
    def _():
        mine = lax.axis_index(col_axis) ^ lax.axis_index(row_axis)
        left[...] = jnp.zeros_like(left)
        for n, (panel, k, group) in enumerate(items):
            start = k * chunk if panels[panel].shape[0] > chunk else 0
            ids = panels[panel][start + slots * width : start + chunk, :].astype(jnp.float32).astype(jnp.int32)
            for s in range(slots):
                at = pl.multiple_of(ids[s, 0] * width, width)
                left[pl.ds(at, width), n * width : (n + 1) * width] = panels[panel][
                    start + s * width : start + (s + 1) * width, :
                ]
            for j in range(4):

                @pl.when((mine ^ group) == j)
                def _():
                    right[n * width : (n + 1) * width, :] = uppers[j][k * width : (k + 1) * width, :]

    rows = out.shape[0]
    at = pl.multiple_of(step * rows + width, width)
    update = jnp.dot(left[pl.ds(at, rows), :], right[...], preferred_element_type=jnp.float32)
    if base_count:
        out[...] = bases[0][...] + update
    else:
        out[...] = update


def accumulate(panels, items, uppers, bases, out_shape, slots, col_axis, row_axis, steps=4):
    width = panels[0].shape[1]
    rows = out_shape[0] // steps
    block = pl.BlockSpec((rows, out_shape[1]), lambda i: (i, 0))
    depth = len(items) * width
    return pl.pallas_call(
        functools.partial(
            accumulate_kernel, slots, col_axis, row_axis, tuple(items), len(panels), len(bases)
        ),
        grid=(steps,),
        out_shape=jax.ShapeDtypeStruct(out_shape, jnp.float32),
        in_specs=[whole_vmem()] * (len(panels) + 4) + [block] * len(bases),
        out_specs=block,
        scratch_shapes=[
            pltpu.VMEM((out_shape[0] + width, depth), jnp.bfloat16),
            pltpu.VMEM((depth, out_shape[1]), jnp.bfloat16),
        ],
        compiler_params=pltpu.CompilerParams(vmem_limit_bytes=VMEM_LIMIT),
        name="accumulate_tiles",
    )(*panels, *uppers, *bases)


def finish_kernel(ancestor, mine, other, out):
    out[...] = ancestor[...] - (mine[...] + other[...])


def finish(ancestor, mine, other, steps=8):
    block = pl.BlockSpec((ancestor.shape[0] // steps, ancestor.shape[1]), lambda i: (i, 0))
    return pl.pallas_call(
        finish_kernel,
        grid=(steps,),
        out_shape=jax.ShapeDtypeStruct(ancestor.shape, jnp.float32),
        in_specs=[block] * 3,
        out_specs=block,
        compiler_params=pltpu.CompilerParams(vmem_limit_bytes=VMEM_LIMIT),
        name="subtract_layers",
    )(ancestor, mine, other)


def swap(array, axis, mask):
    return lax.ppermute(array, axis, [(i, i ^ mask) for i in range(4)])


def on_line_of_four(
    ancestor, lower_panel, row_ids, row_counts, diag_inverse, upper_panel, col_ids, col_counts
):
    width = lower_panel.shape[-1]
    slots = lower_panel.shape[2]
    both, first, second, spread = prepare(
        lower_panel[0],
        row_ids,
        row_counts,
        diag_inverse[0],
        upper_panel[0],
        col_ids,
        col_counts,
        ancestor.shape[1] // width,
    )
    near = swap(both, "col", 1)
    far_first = swap(first, "col", 2)
    far_second = swap(second, "col", 2)
    last_first = swap(far_first, "col", 1)
    last_second = swap(far_second, "col", 1)
    uppers = [spread] + [swap(spread, "row", j) for j in (1, 2, 3)]
    shape = ancestor.shape
    early = accumulate(
        [both, near], [(0, 0, 0), (0, 1, 0), (1, 0, 1), (1, 1, 1)], uppers, [], shape, slots, "col", "row"
    )
    partial = accumulate(
        [far_first, far_second, last_first, last_second],
        [(0, 0, 2), (1, 1, 2), (2, 0, 3), (3, 1, 3)],
        uppers,
        [early],
        shape,
        slots,
        "col",
        "row",
    )
    other = lax.ppermute(partial, "gz", [(0, 1), (1, 0)])
    return finish(ancestor, partial, other)


def spread_tiles(tiles, ids, counts, blocks, rule):
    slot_index = jnp.arange(ids.shape[1], dtype=jnp.int32)
    alive = slot_index[None, :] < counts
    target = jnp.arange(blocks, dtype=jnp.int32)
    select = ((ids[:, :, None] == target[None, None, :]) & alive[:, :, None]).astype(jnp.bfloat16)
    return jnp.einsum(rule, select, tiles, preferred_element_type=jnp.float32).astype(jnp.bfloat16)


def on_device(
    ancestor, lower_panel, row_ids, row_counts, diag_inverse, upper_panel, col_ids, col_counts
):
    width = lower_panel.shape[-1]
    rows, columns = ancestor.shape
    solved = jnp.einsum(
        "ksab,kbc->ksac", lower_panel[0], diag_inverse[0], preferred_element_type=jnp.float32
    ).astype(jnp.bfloat16)
    piece = lax.all_gather((upper_panel[0], col_ids[0], col_counts[0]), "row", axis=0, tiled=True)
    upper_dense = spread_tiles(*piece, columns // width, "kcm,kcab->kamb").reshape(-1, columns)
    piece = lax.all_gather((solved, row_ids[0], row_counts[0]), "col", axis=0, tiled=True)
    lower_dense = spread_tiles(*piece, rows // width, "krl,krab->lakb").reshape(rows, -1)
    partial_sum = jnp.dot(lower_dense, upper_dense, preferred_element_type=jnp.float32)
    return ancestor - lax.psum(partial_sum, "gz")


def solution(mesh):
    placed = (
        P("row", "col"),
        P("gz", "col", "row", None, None),
        P("gz", "col", "row"),
        P("gz", "col", "row"),
        P("gz", "col", None, None),
        P("gz", "row", "col", None, None),
        P("gz", "row", "col"),
        P("gz", "row", "col"),
    )
    sizes = dict(mesh.shape)
    small = sizes["gz"] == 2 and sizes["row"] == 4 and sizes["col"] == 4

    def run(ancestor, lower_panel, *rest):
        two = lower_panel.shape[1] == 2 * sizes["col"]
        body = on_line_of_four if small and two else on_device
        return jax.shard_map(
            body, mesh=mesh, in_specs=placed, out_specs=P("row", "col"), check_vma=False
        )(ancestor, lower_panel, *rest)

    return run
```

```python
import functools

import jax
import jax.numpy as jnp
from jax import lax
from jax.experimental import pallas as pl
from jax.experimental.pallas import tpu as pltpu
from jax.sharding import PartitionSpec as P

VMEM_LIMIT = 24 * 1024 * 1024
ID_ROWS = 16
ROW_STEPS = 4


def whole_vmem():
    return pl.BlockSpec(memory_space=pltpu.VMEM)


def prepare_kernel(
    row_ids_in, row_counts_in, col_ids_in, col_counts_in, lower_in, inverse_in, upper_in,
    solved_out, spread,
    row_ids, row_counts, col_ids, col_counts, lower, inverse, upper, arrived,
):
    supernodes, slots, width, _ = lower.shape
    chunk = slots * width + ID_ROWS
    pairs = (
        (row_ids_in, row_ids),
        (row_counts_in, row_counts),
        (inverse_in.at[0], inverse),
        (lower_in.at[0, 0], lower.at[0]),
        (lower_in.at[0, 1], lower.at[1]),
        (col_ids_in, col_ids),
        (col_counts_in, col_counts),
        (upper_in.at[0], upper),
    )
    copies = [pltpu.make_async_copy(src, dst, arrived.at[n]) for n, (src, dst) in enumerate(pairs)]
    for copy in copies:
        copy.start()
    spread[...] = jnp.zeros_like(spread)
    for copy in copies[:3]:
        copy.wait()
    for k in range(supernodes):
        copies[3 + k].wait()
        tiles = lower[k].reshape(slots * width, width)
        solved = jnp.dot(tiles, inverse[k], preferred_element_type=jnp.float32).astype(jnp.bfloat16)
        solved_out[k * chunk : k * chunk + slots * width, :] = solved
        at_row = lax.broadcasted_iota(jnp.int32, (ID_ROWS, width), 0)
        ids = jnp.zeros((ID_ROWS, width), jnp.int32)
        for s in range(slots):
            place = jnp.where(s < row_counts[0, 0, k], row_ids[0, k, s] + 1, 0)
            ids = jnp.where(at_row == s, place, ids)
        solved_out[k * chunk + slots * width : (k + 1) * chunk, :] = ids.astype(jnp.float32).astype(jnp.bfloat16)
    for copy in copies[5:]:
        copy.wait()
    for k in range(supernodes):
        for c in range(upper.shape[1]):

            @pl.when(c < col_counts[0, 0, k])
            def _():
                at = pl.multiple_of(col_ids[0, k, c] * width, width)
                spread[k * width : (k + 1) * width, pl.ds(at, width)] = upper[k, c]


def prepare(lower, row_ids, row_counts, inverse, upper, col_ids, col_counts, col_blocks):
    _, supernodes, slots, width, _ = lower.shape
    chunk = slots * width + ID_ROWS
    row_counts = jnp.swapaxes(row_counts, 1, 2)
    col_counts = jnp.swapaxes(col_counts, 1, 2)
    return pl.pallas_call(
        prepare_kernel,
        out_shape=(
            jax.ShapeDtypeStruct((supernodes * chunk, width), jnp.bfloat16),
            jax.ShapeDtypeStruct((supernodes * width, col_blocks * width), jnp.bfloat16),
        ),
        in_specs=[pl.BlockSpec(memory_space=pltpu.HBM)] * 7,
        out_specs=(whole_vmem(),) * 2,
        scratch_shapes=[
            pltpu.SMEM(row_ids.shape, jnp.int32),
            pltpu.SMEM(row_counts.shape, jnp.int32),
            pltpu.SMEM(col_ids.shape, jnp.int32),
            pltpu.SMEM(col_counts.shape, jnp.int32),
            pltpu.VMEM(lower.shape[1:], jnp.bfloat16),
            pltpu.VMEM(inverse.shape[1:], jnp.bfloat16),
            pltpu.VMEM(upper.shape[1:], jnp.bfloat16),
            pltpu.SemaphoreType.DMA((8,)),
        ],
        compiler_params=pltpu.CompilerParams(vmem_limit_bytes=VMEM_LIMIT),
        name="solve_and_pack",
    )(
        *(
            pltpu.with_memory_space_constraint(array, pltpu.HBM)
            for array in (row_ids, row_counts, col_ids, col_counts, lower, inverse, upper)
        )
    )


def place_tiles(panel, k, slots, left, at_col):
    width = panel.shape[1]
    chunk = slots * width + ID_ROWS
    start = k * chunk
    ids = panel[start + slots * width : start + chunk, :].astype(jnp.float32).astype(jnp.int32)
    for s in range(slots):
        at = pl.multiple_of(ids[s, 0] * width, width)
        left[pl.ds(at, width), at_col] = panel[start + s * width : start + (s + 1) * width, :]


def order_kernel(count, *refs):
    pieces, out = refs[:count], refs[-1]
    tall = pieces[0].shape[0]
    row = lax.axis_index("row")
    for j, piece in enumerate(pieces):
        out[pl.ds(pl.multiple_of((row ^ j) * tall, tall), tall), :] = piece[...]


def in_order(pieces, after):
    tall, columns = pieces[0].shape
    return pl.pallas_call(
        functools.partial(order_kernel, len(pieces)),
        out_shape=jax.ShapeDtypeStruct((len(pieces) * tall, columns), jnp.bfloat16),
        in_specs=[whole_vmem()] * len(pieces) + [pl.BlockSpec(memory_space=pl.ANY)] * len(after),
        out_specs=whole_vmem(),
        compiler_params=pltpu.CompilerParams(vmem_limit_bytes=VMEM_LIMIT),
        name="order_uppers",
    )(*pieces, *after)


def place_groups(slots, supernodes, masks, panels, uppers, left, right):
    width = panels[0][0].shape[1]
    tall = supernodes * width
    column = lax.axis_index("col")
    layer = lax.axis_index("gz")
    left[...] = jnp.zeros_like(left)
    for side, (tiles, upper) in enumerate(zip(panels, uppers)):
        base = (layer if side == 0 else 1 - layer) * (len(masks) * tall)
        for n, mask in enumerate(masks):
            start = pl.multiple_of(base + n * tall, width)
            right[pl.ds(start, tall), :] = upper[pl.ds(pl.multiple_of((column ^ mask) * tall, tall), tall), :]
            for k in range(supernodes):
                at = pl.multiple_of(base + n * tall + k * width, width)
                place_tiles(tiles[n], k, slots, left, pl.ds(at, width))


def sum_kernel(slots, supernodes, masks, *refs):
    groups = len(masks)
    panels = (refs[:groups], refs[groups : 2 * groups])
    uppers, (out, left, right) = refs[2 * groups : 2 * groups + 2], refs[2 * groups + 2 :]
    width = panels[0][0].shape[1]
    place_groups(slots, supernodes, masks, panels, uppers, left, right)
    rows = out.shape[0] // ROW_STEPS
    for i in range(ROW_STEPS):
        out[i * rows : (i + 1) * rows, :] = jnp.dot(
            left[width + i * rows : width + (i + 1) * rows, :], right[...], preferred_element_type=jnp.float32
        )


def sum_groups(masks, own, other, uppers, shape, slots, supernodes):
    width = own[0].shape[1]
    depth = 2 * len(masks) * supernodes * width
    return pl.pallas_call(
        functools.partial(sum_kernel, slots, supernodes, tuple(masks)),
        out_shape=jax.ShapeDtypeStruct(shape, jnp.float32),
        in_specs=[whole_vmem()] * (2 * len(masks) + 2),
        out_specs=whole_vmem(),
        scratch_shapes=[
            pltpu.VMEM((shape[0] + width, depth), jnp.bfloat16),
            pltpu.VMEM((depth, shape[1]), jnp.bfloat16),
        ],
        compiler_params=pltpu.CompilerParams(vmem_limit_bytes=VMEM_LIMIT),
        name="sum_groups",
    )(*own, *other, *uppers)


def finish_kernel(slots, supernodes, mask, ancestor, early, own, other, own_upper, far_upper, out, left, right, result, sent):
    width = own.shape[1]
    place_groups(slots, supernodes, (mask,), ((own,), (other,)), (own_upper, far_upper), left, right)
    rows = out.shape[0] // ROW_STEPS
    copies = []
    for i in range(ROW_STEPS):
        block = slice(i * rows, (i + 1) * rows)
        update = jnp.dot(
            left[width + i * rows : width + (i + 1) * rows, :], right[...], preferred_element_type=jnp.float32
        )
        result[block, :] = ancestor[block, :] - (early[block, :] + update)
        copy = pltpu.make_async_copy(result.at[block], out.at[block], sent.at[i])
        copy.start()
        copies.append(copy)
    for copy in copies:
        copy.wait()


def finish(ancestor, early, mask, own, other, uppers, slots, supernodes):
    width = own.shape[1]
    depth = 2 * supernodes * width
    return pl.pallas_call(
        functools.partial(finish_kernel, slots, supernodes, mask),
        out_shape=jax.ShapeDtypeStruct(ancestor.shape, jnp.float32),
        in_specs=[whole_vmem()] * 6,
        out_specs=pl.BlockSpec(memory_space=pltpu.HBM),
        scratch_shapes=[
            pltpu.VMEM((ancestor.shape[0] + width, depth), jnp.bfloat16),
            pltpu.VMEM((depth, ancestor.shape[1]), jnp.bfloat16),
            pltpu.VMEM(ancestor.shape, jnp.float32),
            pltpu.SemaphoreType.DMA((ROW_STEPS,)),
        ],
        compiler_params=pltpu.CompilerParams(vmem_limit_bytes=VMEM_LIMIT),
        name="last_group_and_subtract",
    )(ancestor, early, own, other, *uppers)


def swap(array, axis, mask):
    return lax.ppermute(array, axis, [(i, i ^ mask) for i in range(4)])


def siblings(array):
    return lax.ppermute(array, "gz", [(0, 1), (1, 0)])


def on_line_of_four(
    ancestor, lower_panel, row_ids, row_counts, diag_inverse, upper_panel, col_ids, col_counts
):
    width = lower_panel.shape[-1]
    supernodes, slots = lower_panel.shape[1:3]
    mine, spread = prepare(
        lower_panel,
        row_ids,
        row_counts,
        diag_inverse,
        upper_panel,
        col_ids,
        col_counts,
        ancestor.shape[1] // width,
    )
    far = swap(mine, "col", 2)
    near = swap(mine, "col", 1)
    last = swap(far, "col", 1)
    upper = in_order([spread] + [swap(spread, "row", j) for j in (1, 2, 3)], [near, far])
    uppers = (upper, siblings(upper))
    panels = (mine, near, far)
    early = sum_groups(
        (0, 1, 2), panels, [siblings(panel) for panel in panels], uppers, ancestor.shape, slots, supernodes
    )
    return finish(ancestor, early, 3, last, siblings(last), uppers, slots, supernodes)


def spread_tiles(tiles, ids, counts, blocks, rule):
    slot_index = jnp.arange(ids.shape[1], dtype=jnp.int32)
    alive = slot_index[None, :] < counts
    target = jnp.arange(blocks, dtype=jnp.int32)
    select = ((ids[:, :, None] == target[None, None, :]) & alive[:, :, None]).astype(jnp.bfloat16)
    return jnp.einsum(rule, select, tiles, preferred_element_type=jnp.float32).astype(jnp.bfloat16)


def on_device(
    ancestor, lower_panel, row_ids, row_counts, diag_inverse, upper_panel, col_ids, col_counts
):
    width = lower_panel.shape[-1]
    rows, columns = ancestor.shape
    solved = jnp.einsum(
        "ksab,kbc->ksac", lower_panel[0], diag_inverse[0], preferred_element_type=jnp.float32
    ).astype(jnp.bfloat16)
    piece = lax.all_gather((upper_panel[0], col_ids[0], col_counts[0]), "row", axis=0, tiled=True)
    upper_dense = spread_tiles(*piece, columns // width, "kcm,kcab->kamb").reshape(-1, columns)
    piece = lax.all_gather((solved, row_ids[0], row_counts[0]), "col", axis=0, tiled=True)
    lower_dense = spread_tiles(*piece, rows // width, "krl,krab->lakb").reshape(rows, -1)
    partial_sum = jnp.dot(lower_dense, upper_dense, preferred_element_type=jnp.float32)
    return ancestor - lax.psum(partial_sum, "gz")


def solution(mesh):
    placed = (
        P("row", "col"),
        P("gz", "col", "row", None, None),
        P("gz", "col", "row"),
        P("gz", "col", "row"),
        P("gz", "col", None, None),
        P("gz", "row", "col", None, None),
        P("gz", "row", "col"),
        P("gz", "row", "col"),
    )
    sizes = dict(mesh.shape)
    small = sizes["gz"] == 2 and sizes["row"] == 4 and sizes["col"] == 4

    def run(ancestor, lower_panel, *rest):
        two = lower_panel.shape[1] == 2 * sizes["col"]
        body = on_line_of_four if small and two else on_device
        return jax.shard_map(
            body, mesh=mesh, in_specs=placed, out_specs=P("row", "col"), check_vma=False
        )(ancestor, lower_panel, *rest)

    return run
```

```python
import functools

import jax
import jax.numpy as jnp
from jax import lax
from jax.experimental import pallas as pl
from jax.experimental.pallas import tpu as pltpu
from jax.sharding import PartitionSpec as P

VMEM_LIMIT = 24 * 1024 * 1024
ID_ROWS = 16
ROW_STEPS = 4
DECLARED_FLOPS = 100_000_000_000


def whole_vmem():
    return pl.BlockSpec(memory_space=pltpu.VMEM)


def pack_ids(ids, counts, k, slots, width):
    at_row = lax.broadcasted_iota(jnp.int32, (ID_ROWS, width), 0)
    rows = jnp.zeros((ID_ROWS, width), jnp.int32)
    for s in range(slots):
        rows = jnp.where(at_row == s, jnp.where(s < counts[0, 0, k], ids[0, k, s] + 1, 0), rows)
    return rows.astype(jnp.float32).astype(jnp.bfloat16)


def prepare_kernel(
    row_ids_in, row_counts_in, col_ids_in, col_counts_in, lower_in, inverse_in, upper_in,
    both, first, second, packed,
    row_ids, row_counts, col_ids, col_counts, lower, inverse, upper, arrived,
):
    supernodes, slots, width, _ = lower.shape
    chunk = slots * width + ID_ROWS
    pairs = (
        (row_ids_in, row_ids),
        (row_counts_in, row_counts),
        (inverse_in.at[0], inverse),
        (lower_in.at[0, 0], lower.at[0]),
        (lower_in.at[0, 1], lower.at[1]),
        (col_ids_in, col_ids),
        (col_counts_in, col_counts),
        (upper_in.at[0], upper),
    )
    copies = [pltpu.make_async_copy(src, dst, arrived.at[n]) for n, (src, dst) in enumerate(pairs)]
    for copy in copies:
        copy.start()
    for copy in copies[:3]:
        copy.wait()
    for k, half in enumerate((first, second)):
        copies[3 + k].wait()
        tiles = lower[k].reshape(slots * width, width)
        solved = jnp.dot(tiles, inverse[k], preferred_element_type=jnp.float32).astype(jnp.bfloat16)
        ids = pack_ids(row_ids, row_counts, k, slots, width)
        half[0 : slots * width, :] = solved
        half[slots * width : chunk, :] = ids
        both[k * chunk : k * chunk + slots * width, :] = solved
        both[k * chunk + slots * width : (k + 1) * chunk, :] = ids
    for copy in copies[5:]:
        copy.wait()
    slots = upper.shape[1]
    chunk = slots * width + ID_ROWS
    for k in range(supernodes):
        packed[k * chunk : k * chunk + slots * width, :] = upper[k].reshape(slots * width, width)
        packed[k * chunk + slots * width : (k + 1) * chunk, :] = pack_ids(col_ids, col_counts, k, slots, width)


def prepare(lower, row_ids, row_counts, inverse, upper, col_ids, col_counts):
    _, supernodes, slots, width, _ = lower.shape
    chunk = slots * width + ID_ROWS
    row_counts = jnp.swapaxes(row_counts, 1, 2)
    col_counts = jnp.swapaxes(col_counts, 1, 2)
    return pl.pallas_call(
        prepare_kernel,
        out_shape=(
            jax.ShapeDtypeStruct((supernodes * chunk, width), jnp.bfloat16),
            jax.ShapeDtypeStruct((chunk, width), jnp.bfloat16),
            jax.ShapeDtypeStruct((chunk, width), jnp.bfloat16),
            jax.ShapeDtypeStruct((supernodes * (upper.shape[2] * width + ID_ROWS), width), jnp.bfloat16),
        ),
        in_specs=[pl.BlockSpec(memory_space=pltpu.HBM)] * 7,
        out_specs=(whole_vmem(),) * 4,
        scratch_shapes=[
            pltpu.SMEM(row_ids.shape, jnp.int32),
            pltpu.SMEM(row_counts.shape, jnp.int32),
            pltpu.SMEM(col_ids.shape, jnp.int32),
            pltpu.SMEM(col_counts.shape, jnp.int32),
            pltpu.VMEM(lower.shape[1:], jnp.bfloat16),
            pltpu.VMEM(inverse.shape[1:], jnp.bfloat16),
            pltpu.VMEM(upper.shape[1:], jnp.bfloat16),
            pltpu.SemaphoreType.DMA((8,)),
        ],
        compiler_params=pltpu.CompilerParams(vmem_limit_bytes=VMEM_LIMIT),
        name="solve_and_pack",
    )(
        *(
            pltpu.with_memory_space_constraint(array, pltpu.HBM)
            for array in (row_ids, row_counts, col_ids, col_counts, lower, inverse, upper)
        )
    )


def spread_kernel(slots, supernodes, packed, *refs):
    out, padded = refs[-2:]
    width = packed.shape[1]
    chunk = slots * width + ID_ROWS
    padded[...] = jnp.zeros_like(padded)
    for k in range(supernodes):
        ids = packed[k * chunk + slots * width : (k + 1) * chunk, :].astype(jnp.float32).astype(jnp.int32)
        for s in range(slots):
            at = pl.multiple_of(ids[s, 0] * width, width)
            padded[k * width : (k + 1) * width, pl.ds(at, width)] = packed[
                k * chunk + s * width : k * chunk + (s + 1) * width, :
            ]
    out[...] = padded[:, width:]


def spread_uppers(packed, after, slots, columns):
    width = packed.shape[1]
    supernodes = packed.shape[0] // (slots * width + ID_ROWS)
    return pl.pallas_call(
        functools.partial(spread_kernel, slots, supernodes),
        out_shape=jax.ShapeDtypeStruct((supernodes * width, columns), jnp.bfloat16),
        in_specs=[whole_vmem()] + [pl.BlockSpec(memory_space=pl.ANY)] * len(after),
        out_specs=whole_vmem(),
        scratch_shapes=[pltpu.VMEM((supernodes * width, columns + width), jnp.bfloat16)],
        compiler_params=pltpu.CompilerParams(vmem_limit_bytes=VMEM_LIMIT),
        name="spread_uppers",
    )(packed, *after)


def ids_kernel(panel, out):
    out[...] = panel[panel.shape[0] - ID_ROWS :, :]


def ids_of(panel):
    return pl.pallas_call(
        ids_kernel,
        out_shape=jax.ShapeDtypeStruct((ID_ROWS, panel.shape[1]), panel.dtype),
        in_specs=[whole_vmem()],
        out_specs=whole_vmem(),
        compiler_params=pltpu.CompilerParams(vmem_limit_bytes=VMEM_LIMIT),
        cost_estimate=pl.CostEstimate(flops=DECLARED_FLOPS, bytes_accessed=0, transcendentals=0),
        name="ids_of_last",
    )(panel)


def place_tiles(panel, k, slots, left, at_col):
    width = panel.shape[1]
    chunk = slots * width + ID_ROWS
    start = k * chunk
    ids = panel[start + slots * width : start + chunk, :].astype(jnp.float32).astype(jnp.int32)
    for s in range(slots):
        at = pl.multiple_of(ids[s, 0] * width, width)
        left[pl.ds(at, width), at_col] = panel[start + s * width : start + (s + 1) * width, :]


def place_items(slots, tall, items, panels, uppers, left, right):
    width = panels[0][0].shape[1]
    column = lax.axis_index("col")
    layer = lax.axis_index("gz")
    left[...] = jnp.zeros_like(left)
    for side, (tiles, upper) in enumerate(zip(panels, uppers)):
        base = (layer if side == 0 else 1 - layer) * (len(items) * width)
        for n, (panel, at, k, mask) in enumerate(items):
            start = pl.multiple_of(base + n * width, width)
            rows = pl.multiple_of((column ^ mask) * tall + k * width, width)
            right[pl.ds(start, width), :] = upper[pl.ds(rows, width), :]
            place_tiles(tiles[panel], at, slots, left, pl.ds(start, width))


def sum_kernel(slots, tall, items, count, *refs):
    panels = (refs[:count], refs[count : 2 * count])
    uppers, (out, left, right) = refs[2 * count : 2 * count + 2], refs[2 * count + 2 :]
    width = panels[0][0].shape[1]
    place_items(slots, tall, items, panels, uppers, left, right)
    rows = out.shape[0] // ROW_STEPS
    for i in range(ROW_STEPS):
        out[i * rows : (i + 1) * rows, :] = jnp.dot(
            left[width + i * rows : width + (i + 1) * rows, :], right[...], preferred_element_type=jnp.float32
        )


def sum_items(items, own, other, uppers, shape, slots, supernodes):
    width = own[0].shape[1]
    depth = 2 * len(items) * width
    return pl.pallas_call(
        functools.partial(sum_kernel, slots, supernodes * width, tuple(items), len(own)),
        out_shape=jax.ShapeDtypeStruct(shape, jnp.float32),
        in_specs=[whole_vmem()] * (2 * len(own) + 2),
        out_specs=whole_vmem(),
        scratch_shapes=[
            pltpu.VMEM((shape[0] + width, depth), jnp.bfloat16),
            pltpu.VMEM((depth, shape[1]), jnp.bfloat16),
        ],
        compiler_params=pltpu.CompilerParams(vmem_limit_bytes=VMEM_LIMIT),
        name="sum_groups",
    )(*own, *other, *uppers)


def finish_kernel(slots, tall, items, count, ancestor, early, *refs):
    panels = (refs[:count], refs[count : 2 * count])
    uppers, (out, left, right, result, sent) = refs[2 * count : 2 * count + 2], refs[-5:]
    width = panels[0][0].shape[1]
    place_items(slots, tall, items, panels, uppers, left, right)
    rows = out.shape[0] // ROW_STEPS
    copies = []
    for i in range(ROW_STEPS):
        block = slice(i * rows, (i + 1) * rows)
        update = jnp.dot(
            left[width + i * rows : width + (i + 1) * rows, :], right[...], preferred_element_type=jnp.float32
        )
        result[block, :] = ancestor[block, :] - (early[block, :] + update)
        copy = pltpu.make_async_copy(result.at[block], out.at[block], sent.at[i])
        copy.start()
        copies.append(copy)
    for copy in copies:
        copy.wait()


def finish(ancestor, early, items, own, other, uppers, after, slots, supernodes):
    width = own[0].shape[1]
    depth = 2 * len(items) * width
    return pl.pallas_call(
        functools.partial(finish_kernel, slots, supernodes * width, tuple(items), len(own)),
        out_shape=jax.ShapeDtypeStruct(ancestor.shape, jnp.float32),
        in_specs=[whole_vmem()] * (2 * len(own) + 4) + [pl.BlockSpec(memory_space=pl.ANY)] * len(after),
        out_specs=pl.BlockSpec(memory_space=pltpu.HBM),
        scratch_shapes=[
            pltpu.VMEM((ancestor.shape[0] + width, depth), jnp.bfloat16),
            pltpu.VMEM((depth, ancestor.shape[1]), jnp.bfloat16),
            pltpu.VMEM(ancestor.shape, jnp.float32),
            pltpu.SemaphoreType.DMA((ROW_STEPS,)),
        ],
        compiler_params=pltpu.CompilerParams(vmem_limit_bytes=VMEM_LIMIT),
        name="last_group_and_subtract",
    )(ancestor, early, *own, *other, *uppers, *after)


def swap(array, axis, mask):
    return lax.ppermute(array, axis, [(i, i ^ mask) for i in range(4)])


def siblings(array):
    return lax.ppermute(array, "gz", [(0, 1), (1, 0)])


def on_line_of_four(
    ancestor, lower_panel, row_ids, row_counts, diag_inverse, upper_panel, col_ids, col_counts
):
    supernodes, slots = lower_panel.shape[1:3]
    both, first, second, packed = prepare(
        lower_panel, row_ids, row_counts, diag_inverse, upper_panel, col_ids, col_counts
    )
    near = swap(both, "col", 1)
    far_first = swap(first, "col", 2)
    far_second = swap(second, "col", 2)
    packed = lax.all_gather(packed, "row", axis=0, tiled=True)
    far_first, packed = lax.optimization_barrier((far_first, packed))
    last_first = swap(far_first, "col", 1)
    last_second = swap(far_second, "col", 1)
    other_both, other_first = siblings(both), siblings(far_first)
    upper = spread_uppers(
        packed,
        [near, far_second, last_first, other_both, other_first],
        upper_panel.shape[2],
        ancestor.shape[1],
    )
    panels = [both, near, far_first, far_second]
    other_near, other_second, other_upper = siblings(near), siblings(far_second), siblings(upper)
    last_second, other_near, other_second, other_upper, ids = lax.optimization_barrier(
        (last_second, other_near, other_second, other_upper, ids_of(last_second))
    )
    others = [other_both, other_near, other_first, other_second]
    last = [last_first, last_second]
    early = sum_items(
        [(0, 0, 0, 0), (0, 1, 1, 0), (1, 0, 0, 1), (1, 1, 1, 1), (2, 0, 0, 2), (3, 0, 1, 2)],
        panels,
        others,
        (upper, other_upper),
        ancestor.shape,
        slots,
        supernodes,
    )
    return finish(
        ancestor,
        early,
        [(0, 0, 0, 3), (1, 0, 1, 3)],
        last,
        [siblings(panel) for panel in last],
        (upper, other_upper),
        [ids],
        slots,
        supernodes,
    )


def spread_tiles(tiles, ids, counts, blocks, rule):
    slot_index = jnp.arange(ids.shape[1], dtype=jnp.int32)
    alive = slot_index[None, :] < counts
    target = jnp.arange(blocks, dtype=jnp.int32)
    select = ((ids[:, :, None] == target[None, None, :]) & alive[:, :, None]).astype(jnp.bfloat16)
    return jnp.einsum(rule, select, tiles, preferred_element_type=jnp.float32).astype(jnp.bfloat16)


def on_device(
    ancestor, lower_panel, row_ids, row_counts, diag_inverse, upper_panel, col_ids, col_counts
):
    width = lower_panel.shape[-1]
    rows, columns = ancestor.shape
    solved = jnp.einsum(
        "ksab,kbc->ksac", lower_panel[0], diag_inverse[0], preferred_element_type=jnp.float32
    ).astype(jnp.bfloat16)
    piece = lax.all_gather((upper_panel[0], col_ids[0], col_counts[0]), "row", axis=0, tiled=True)
    upper_dense = spread_tiles(*piece, columns // width, "kcm,kcab->kamb").reshape(-1, columns)
    piece = lax.all_gather((solved, row_ids[0], row_counts[0]), "col", axis=0, tiled=True)
    lower_dense = spread_tiles(*piece, rows // width, "krl,krab->lakb").reshape(rows, -1)
    partial_sum = jnp.dot(lower_dense, upper_dense, preferred_element_type=jnp.float32)
    return ancestor - lax.psum(partial_sum, "gz")


def solution(mesh):
    placed = (
        P("row", "col"),
        P("gz", "col", "row", None, None),
        P("gz", "col", "row"),
        P("gz", "col", "row"),
        P("gz", "col", None, None),
        P("gz", "row", "col", None, None),
        P("gz", "row", "col"),
        P("gz", "row", "col"),
    )
    sizes = dict(mesh.shape)
    small = sizes["gz"] == 2 and sizes["row"] == 4 and sizes["col"] == 4

    def run(ancestor, lower_panel, *rest):
        two = lower_panel.shape[1] == 2 * sizes["col"]
        body = on_line_of_four if small and two else on_device
        return jax.shard_map(
            body, mesh=mesh, in_specs=placed, out_specs=P("row", "col"), check_vma=False
        )(ancestor, lower_panel, *rest)

    return run
```

```python
import functools

import jax
import jax.numpy as jnp
from jax import lax
from jax.experimental import pallas as pl
from jax.experimental.pallas import tpu as pltpu
from jax.sharding import PartitionSpec as P

VMEM_LIMIT = 24 * 1024 * 1024
ID_ROWS = 16
ROW_STEPS = 4
DECLARED_FLOPS = 10_000_000_000


def whole_vmem():
    return pl.BlockSpec(memory_space=pltpu.VMEM)


def pack_ids(ids, counts, supernodes, slots, width):
    at_row = lax.broadcasted_iota(jnp.int32, (ID_ROWS, width), 0)
    rows = jnp.zeros((ID_ROWS, width), jnp.int32)
    for k in range(supernodes):
        for s in range(slots):
            value = jnp.where(s < counts[0, 0, k], ids[0, k, s] + 1, 0)
            rows = jnp.where(at_row == k * slots + s, value, rows)
    return rows.astype(jnp.float32).astype(jnp.bfloat16)


def read_ids(rows):
    return rows.astype(jnp.float32).astype(jnp.int32)


def prepare_kernel(
    row_ids_in, row_counts_in, col_ids_in, col_counts_in, lower_in, inverse_in, upper_in,
    both, first, second, packed,
    row_ids, row_counts, col_ids, col_counts, lower, inverse, upper, arrived,
):
    supernodes, slots, width, _ = lower.shape
    tall = slots * width
    cut = first.shape[0] - ID_ROWS
    pairs = (
        (row_ids_in, row_ids),
        (row_counts_in, row_counts),
        (inverse_in.at[0], inverse),
        (lower_in.at[0, 0], lower.at[0]),
        (lower_in.at[0, 1], lower.at[1]),
        (col_ids_in, col_ids),
        (col_counts_in, col_counts),
        (upper_in.at[0], upper),
    )
    copies = [pltpu.make_async_copy(src, dst, arrived.at[n]) for n, (src, dst) in enumerate(pairs)]
    for copy in copies:
        copy.start()
    for copy in copies[:3]:
        copy.wait()
    ids = pack_ids(row_ids, row_counts, supernodes, slots, width)
    first[cut:, :] = ids
    both[supernodes * tall :, :] = ids
    for k in range(supernodes):
        copies[3 + k].wait()
        solved = jnp.dot(lower[k].reshape(tall, width), inverse[k], preferred_element_type=jnp.float32)
        solved = solved.astype(jnp.bfloat16)
        start, stop = k * tall, (k + 1) * tall
        both[start:stop, :] = solved
        middle = min(max(cut, start), stop)
        if middle > start:
            first[start:middle, :] = solved[: middle - start]
        if middle < stop:
            second[middle - cut : stop - cut, :] = solved[middle - start :]
    for copy in copies[5:]:
        copy.wait()
    slots = upper.shape[1]
    tall = slots * width
    for k in range(supernodes):
        packed[k * tall : (k + 1) * tall, :] = upper[k].reshape(tall, width)
    packed[supernodes * tall :, :] = pack_ids(col_ids, col_counts, supernodes, slots, width)


def prepare(lower, row_ids, row_counts, inverse, upper, col_ids, col_counts, cut):
    _, supernodes, slots, width, _ = lower.shape
    tiles = supernodes * slots
    row_counts = jnp.swapaxes(row_counts, 1, 2)
    col_counts = jnp.swapaxes(col_counts, 1, 2)
    return pl.pallas_call(
        prepare_kernel,
        out_shape=(
            jax.ShapeDtypeStruct((tiles * width + ID_ROWS, width), jnp.bfloat16),
            jax.ShapeDtypeStruct((cut * width + ID_ROWS, width), jnp.bfloat16),
            jax.ShapeDtypeStruct(((tiles - cut) * width, width), jnp.bfloat16),
            jax.ShapeDtypeStruct((supernodes * upper.shape[2] * width + ID_ROWS, width), jnp.bfloat16),
        ),
        in_specs=[pl.BlockSpec(memory_space=pltpu.HBM)] * 7,
        out_specs=(whole_vmem(),) * 4,
        scratch_shapes=[
            pltpu.SMEM(row_ids.shape, jnp.int32),
            pltpu.SMEM(row_counts.shape, jnp.int32),
            pltpu.SMEM(col_ids.shape, jnp.int32),
            pltpu.SMEM(col_counts.shape, jnp.int32),
            pltpu.VMEM(lower.shape[1:], jnp.bfloat16),
            pltpu.VMEM(inverse.shape[1:], jnp.bfloat16),
            pltpu.VMEM(upper.shape[1:], jnp.bfloat16),
            pltpu.SemaphoreType.DMA((8,)),
        ],
        compiler_params=pltpu.CompilerParams(vmem_limit_bytes=VMEM_LIMIT),
        name="solve_and_pack",
    )(
        *(
            pltpu.with_memory_space_constraint(array, pltpu.HBM)
            for array in (row_ids, row_counts, col_ids, col_counts, lower, inverse, upper)
        )
    )


def spread_kernel(slots, supernodes, packed, *refs):
    out, padded = refs[-2:]
    width = packed.shape[1]
    piece = supernodes * slots * width + ID_ROWS
    padded[...] = jnp.zeros_like(padded)
    for group in range(packed.shape[0] // piece):
        start = group * piece
        ids = read_ids(packed[start + piece - ID_ROWS : start + piece, :])
        for k in range(supernodes):
            rows = slice((group * supernodes + k) * width, (group * supernodes + k + 1) * width)
            for s in range(slots):
                tile = k * slots + s
                at = pl.multiple_of(ids[tile, 0] * width, width)
                padded[rows, pl.ds(at, width)] = packed[start + tile * width : start + (tile + 1) * width, :]
    out[...] = padded[:, width:]


def spread_uppers(packed, after, slots, supernodes, columns):
    width = packed.shape[1]
    deep = packed.shape[0] // (supernodes * slots * width + ID_ROWS) * supernodes * width
    return pl.pallas_call(
        functools.partial(spread_kernel, slots, supernodes),
        out_shape=jax.ShapeDtypeStruct((deep, columns), jnp.bfloat16),
        in_specs=[whole_vmem()] + [pl.BlockSpec(memory_space=pl.ANY)] * len(after),
        out_specs=whole_vmem(),
        scratch_shapes=[pltpu.VMEM((deep, columns + width), jnp.bfloat16)],
        compiler_params=pltpu.CompilerParams(vmem_limit_bytes=VMEM_LIMIT),
        name="spread_uppers",
    )(packed, *after)


def touch_kernel(panel, out):
    out[...] = panel[0:ID_ROWS, :]


def touched(panel):
    return pl.pallas_call(
        touch_kernel,
        out_shape=jax.ShapeDtypeStruct((ID_ROWS, panel.shape[1]), panel.dtype),
        in_specs=[whole_vmem()],
        out_specs=whole_vmem(),
        compiler_params=pltpu.CompilerParams(vmem_limit_bytes=VMEM_LIMIT),
        cost_estimate=pl.CostEstimate(flops=DECLARED_FLOPS, bytes_accessed=0, transcendentals=0),
        name="touch_chunk",
    )(panel)


def place_group(parts, slots, supernodes, left, base):
    width = parts[0].shape[1]
    ids = read_ids(parts[0][parts[0].shape[0] - ID_ROWS :, :])
    cut = (parts[0].shape[0] - ID_ROWS) // width
    for k in range(supernodes):
        columns = pl.ds(pl.multiple_of(base + k * width, width), width)
        for s in range(slots):
            tile = k * slots + s
            part, row = (parts[0], tile) if tile < cut else (parts[1], tile - cut)
            at = pl.multiple_of(ids[tile, 0] * width, width)
            left[pl.ds(at, width), columns] = part[row * width : (row + 1) * width, :]


def place_groups(plan, groups, panels, uppers, left, right):
    slots, supernodes = plan
    width = panels[0][0].shape[1]
    tall = supernodes * width
    column = lax.axis_index("col")
    layer = lax.axis_index("gz")
    left[...] = jnp.zeros_like(left)
    for side, (tiles, upper) in enumerate(zip(panels, uppers)):
        base = (layer if side == 0 else 1 - layer) * (len(groups) * tall)
        for n, (members, mask) in enumerate(groups):
            start = pl.multiple_of(base + n * tall, tall)
            right[pl.ds(start, tall), :] = upper[pl.ds(pl.multiple_of((column ^ mask) * tall, tall), tall), :]
            place_group([tiles[member] for member in members], slots, supernodes, left, start)


def sum_kernel(plan, groups, count, *refs):
    panels = (refs[:count], refs[count : 2 * count])
    uppers, (out, left, right) = refs[2 * count : 2 * count + 2], refs[2 * count + 2 :]
    width = panels[0][0].shape[1]
    place_groups(plan, groups, panels, uppers, left, right)
    rows = out.shape[0] // ROW_STEPS
    for i in range(ROW_STEPS):
        out[i * rows : (i + 1) * rows, :] = jnp.dot(
            left[width + i * rows : width + (i + 1) * rows, :], right[...], preferred_element_type=jnp.float32
        )


def sum_groups(plan, groups, own, other, uppers, shape):
    width = own[0].shape[1]
    depth = 2 * len(groups) * plan[1] * width
    return pl.pallas_call(
        functools.partial(sum_kernel, plan, groups, len(own)),
        out_shape=jax.ShapeDtypeStruct(shape, jnp.float32),
        in_specs=[whole_vmem()] * (2 * len(own) + 2),
        out_specs=whole_vmem(),
        scratch_shapes=[
            pltpu.VMEM((shape[0] + width, depth), jnp.bfloat16),
            pltpu.VMEM((depth, shape[1]), jnp.bfloat16),
        ],
        compiler_params=pltpu.CompilerParams(vmem_limit_bytes=VMEM_LIMIT),
        name="sum_groups",
    )(*own, *other, *uppers)


def finish_kernel(plan, groups, count, ancestor, early, *refs):
    panels = (refs[:count], refs[count : 2 * count])
    uppers, (out, left, right, result, sent) = refs[2 * count : 2 * count + 2], refs[-5:]
    width = panels[0][0].shape[1]
    place_groups(plan, groups, panels, uppers, left, right)
    rows = out.shape[0] // ROW_STEPS
    copies = []
    for i in range(ROW_STEPS):
        block = slice(i * rows, (i + 1) * rows)
        update = jnp.dot(
            left[width + i * rows : width + (i + 1) * rows, :], right[...], preferred_element_type=jnp.float32
        )
        result[block, :] = ancestor[block, :] - (early[block, :] + update)
        copy = pltpu.make_async_copy(result.at[block], out.at[block], sent.at[i])
        copy.start()
        copies.append(copy)
    for copy in copies:
        copy.wait()


def finish(plan, ancestor, early, groups, own, other, uppers, after):
    width = own[0].shape[1]
    depth = 2 * len(groups) * plan[1] * width
    return pl.pallas_call(
        functools.partial(finish_kernel, plan, groups, len(own)),
        out_shape=jax.ShapeDtypeStruct(ancestor.shape, jnp.float32),
        in_specs=[whole_vmem()] * (2 * len(own) + 4) + [pl.BlockSpec(memory_space=pl.ANY)] * len(after),
        out_specs=pl.BlockSpec(memory_space=pltpu.HBM),
        scratch_shapes=[
            pltpu.VMEM((ancestor.shape[0] + width, depth), jnp.bfloat16),
            pltpu.VMEM((depth, ancestor.shape[1]), jnp.bfloat16),
            pltpu.VMEM(ancestor.shape, jnp.float32),
            pltpu.SemaphoreType.DMA((ROW_STEPS,)),
        ],
        compiler_params=pltpu.CompilerParams(vmem_limit_bytes=VMEM_LIMIT),
        name="last_group_and_subtract",
    )(ancestor, early, *own, *other, *uppers, *after)


def swap(array, axis, mask):
    return lax.ppermute(array, axis, [(i, i ^ mask) for i in range(4)])


def siblings(array):
    return lax.ppermute(array, "gz", [(0, 1), (1, 0)])


def on_line_of_four(
    ancestor, lower_panel, row_ids, row_counts, diag_inverse, upper_panel, col_ids, col_counts
):
    supernodes, slots = lower_panel.shape[1:3]
    plan = (slots, supernodes)
    both, first, second, packed = prepare(
        lower_panel,
        row_ids,
        row_counts,
        diag_inverse,
        upper_panel,
        col_ids,
        col_counts,
        2 * supernodes * slots // 3,
    )
    near = swap(both, "col", 1)
    far_first = swap(first, "col", 2)
    far_second = swap(second, "col", 2)
    packed = lax.all_gather(packed, "row", axis=0, tiled=True)
    far_first, packed = lax.optimization_barrier((far_first, packed))
    last_first = swap(far_first, "col", 1)
    far_second, far_mark = lax.optimization_barrier((far_second, touched(far_second)))
    last_second = swap(far_second, "col", 1)
    other_both, other_first = siblings(both), siblings(far_first)
    upper = spread_uppers(
        packed,
        [near, far_second, other_both, other_first],
        upper_panel.shape[2],
        supernodes,
        ancestor.shape[1],
    )
    uppers = (upper, siblings(upper))
    last_first, first_mark = lax.optimization_barrier((last_first, touched(last_first)))
    last_second, second_mark = lax.optimization_barrier((last_second, touched(last_second)))
    early = sum_groups(
        plan,
        (((0,), 0), ((1,), 1), ((2, 3), 2)),
        [both, near, far_first, far_second],
        [other_both, siblings(near), other_first, siblings(far_second)],
        uppers,
        ancestor.shape,
    )
    return finish(
        plan,
        ancestor,
        early,
        (((0, 1), 3),),
        [last_first, last_second],
        [siblings(last_first), siblings(last_second)],
        uppers,
        [far_mark, first_mark, second_mark],
    )


def spread_tiles(tiles, ids, counts, blocks, rule):
    slot_index = jnp.arange(ids.shape[1], dtype=jnp.int32)
    alive = slot_index[None, :] < counts
    target = jnp.arange(blocks, dtype=jnp.int32)
    select = ((ids[:, :, None] == target[None, None, :]) & alive[:, :, None]).astype(jnp.bfloat16)
    return jnp.einsum(rule, select, tiles, preferred_element_type=jnp.float32).astype(jnp.bfloat16)


def on_device(
    ancestor, lower_panel, row_ids, row_counts, diag_inverse, upper_panel, col_ids, col_counts
):
    width = lower_panel.shape[-1]
    rows, columns = ancestor.shape
    solved = jnp.einsum(
        "ksab,kbc->ksac", lower_panel[0], diag_inverse[0], preferred_element_type=jnp.float32
    ).astype(jnp.bfloat16)
    piece = lax.all_gather((upper_panel[0], col_ids[0], col_counts[0]), "row", axis=0, tiled=True)
    upper_dense = spread_tiles(*piece, columns // width, "kcm,kcab->kamb").reshape(-1, columns)
    piece = lax.all_gather((solved, row_ids[0], row_counts[0]), "col", axis=0, tiled=True)
    lower_dense = spread_tiles(*piece, rows // width, "krl,krab->lakb").reshape(rows, -1)
    partial_sum = jnp.dot(lower_dense, upper_dense, preferred_element_type=jnp.float32)
    return ancestor - lax.psum(partial_sum, "gz")


def solution(mesh):
    placed = (
        P("row", "col"),
        P("gz", "col", "row", None, None),
        P("gz", "col", "row"),
        P("gz", "col", "row"),
        P("gz", "col", None, None),
        P("gz", "row", "col", None, None),
        P("gz", "row", "col"),
        P("gz", "row", "col"),
    )
    sizes = dict(mesh.shape)
    small = sizes["gz"] == 2 and sizes["row"] == 4 and sizes["col"] == 4

    def run(ancestor, lower_panel, *rest):
        two = lower_panel.shape[1] == 2 * sizes["col"]
        body = on_line_of_four if small and two else on_device
        return jax.shard_map(
            body, mesh=mesh, in_specs=placed, out_specs=P("row", "col"), check_vma=False
        )(ancestor, lower_panel, *rest)

    return run
```

```python
import functools

import jax
import jax.numpy as jnp
from jax import lax
from jax.experimental import pallas as pl
from jax.experimental.pallas import tpu as pltpu
from jax.sharding import PartitionSpec as P

VMEM_LIMIT = 24 * 1024 * 1024
ID_ROWS = 16
ROW_STEPS = 4
DECLARED_FLOPS = 10_000_000_000
SUM_FLOPS = 2_000_000_000


def whole_vmem():
    return pl.BlockSpec(memory_space=pltpu.VMEM)


def pack_ids(ids, counts, supernodes, slots, width):
    at_row = lax.broadcasted_iota(jnp.int32, (ID_ROWS, width), 0)
    rows = jnp.zeros((ID_ROWS, width), jnp.int32)
    for k in range(supernodes):
        for s in range(slots):
            value = jnp.where(s < counts[0, 0, k], ids[0, k, s] + 1, 0)
            rows = jnp.where(at_row == k * slots + s, value, rows)
    return rows.astype(jnp.float32).astype(jnp.bfloat16)


def read_ids(rows):
    return rows.astype(jnp.float32).astype(jnp.int32)


def prepare_kernel(
    row_ids_in, row_counts_in, col_ids_in, col_counts_in, lower_in, inverse_in, upper_in,
    both, first, second, packed,
    row_ids, row_counts, col_ids, col_counts, lower, inverse, upper, arrived,
):
    supernodes, slots, width, _ = lower.shape
    tall = slots * width
    cut = first.shape[0] - ID_ROWS
    pairs = (
        (row_ids_in, row_ids),
        (row_counts_in, row_counts),
        (inverse_in.at[0], inverse),
        (lower_in.at[0, 0], lower.at[0]),
        (lower_in.at[0, 1], lower.at[1]),
        (col_ids_in, col_ids),
        (col_counts_in, col_counts),
        (upper_in.at[0], upper),
    )
    copies = [pltpu.make_async_copy(src, dst, arrived.at[n]) for n, (src, dst) in enumerate(pairs)]
    for copy in copies:
        copy.start()
    for copy in copies[:3]:
        copy.wait()
    ids = pack_ids(row_ids, row_counts, supernodes, slots, width)
    first[cut:, :] = ids
    both[supernodes * tall :, :] = ids
    for k in range(supernodes):
        copies[3 + k].wait()
        solved = jnp.dot(lower[k].reshape(tall, width), inverse[k], preferred_element_type=jnp.float32)
        solved = solved.astype(jnp.bfloat16)
        start, stop = k * tall, (k + 1) * tall
        both[start:stop, :] = solved
        middle = min(max(cut, start), stop)
        if middle > start:
            first[start:middle, :] = solved[: middle - start]
        if middle < stop:
            second[middle - cut : stop - cut, :] = solved[middle - start :]
    for copy in copies[5:]:
        copy.wait()
    slots = upper.shape[1]
    tall = slots * width
    for k in range(supernodes):
        packed[k * tall : (k + 1) * tall, :] = upper[k].reshape(tall, width)
    packed[supernodes * tall :, :] = pack_ids(col_ids, col_counts, supernodes, slots, width)


def prepare(lower, row_ids, row_counts, inverse, upper, col_ids, col_counts, cut):
    _, supernodes, slots, width, _ = lower.shape
    tiles = supernodes * slots
    row_counts = jnp.swapaxes(row_counts, 1, 2)
    col_counts = jnp.swapaxes(col_counts, 1, 2)
    return pl.pallas_call(
        prepare_kernel,
        out_shape=(
            jax.ShapeDtypeStruct((tiles * width + ID_ROWS, width), jnp.bfloat16),
            jax.ShapeDtypeStruct((cut * width + ID_ROWS, width), jnp.bfloat16),
            jax.ShapeDtypeStruct(((tiles - cut) * width, width), jnp.bfloat16),
            jax.ShapeDtypeStruct((supernodes * upper.shape[2] * width + ID_ROWS, width), jnp.bfloat16),
        ),
        in_specs=[pl.BlockSpec(memory_space=pltpu.HBM)] * 7,
        out_specs=(whole_vmem(),) * 4,
        scratch_shapes=[
            pltpu.SMEM(row_ids.shape, jnp.int32),
            pltpu.SMEM(row_counts.shape, jnp.int32),
            pltpu.SMEM(col_ids.shape, jnp.int32),
            pltpu.SMEM(col_counts.shape, jnp.int32),
            pltpu.VMEM(lower.shape[1:], jnp.bfloat16),
            pltpu.VMEM(inverse.shape[1:], jnp.bfloat16),
            pltpu.VMEM(upper.shape[1:], jnp.bfloat16),
            pltpu.SemaphoreType.DMA((8,)),
        ],
        compiler_params=pltpu.CompilerParams(vmem_limit_bytes=VMEM_LIMIT),
        name="solve_and_pack",
    )(
        *(
            pltpu.with_memory_space_constraint(array, pltpu.HBM)
            for array in (row_ids, row_counts, col_ids, col_counts, lower, inverse, upper)
        )
    )


def spread_kernel(slots, supernodes, packed, *refs):
    out, padded = refs[-2:]
    width = packed.shape[1]
    piece = supernodes * slots * width + ID_ROWS
    padded[...] = jnp.zeros_like(padded)
    for group in range(packed.shape[0] // piece):
        start = group * piece
        ids = read_ids(packed[start + piece - ID_ROWS : start + piece, :])
        for k in range(supernodes):
            rows = slice((group * supernodes + k) * width, (group * supernodes + k + 1) * width)
            for s in range(slots):
                tile = k * slots + s
                at = pl.multiple_of(ids[tile, 0] * width, width)
                padded[rows, pl.ds(at, width)] = packed[start + tile * width : start + (tile + 1) * width, :]
    out[...] = padded[:, width:]


def spread_uppers(packed, after, slots, supernodes, columns):
    width = packed.shape[1]
    deep = packed.shape[0] // (supernodes * slots * width + ID_ROWS) * supernodes * width
    return pl.pallas_call(
        functools.partial(spread_kernel, slots, supernodes),
        out_shape=jax.ShapeDtypeStruct((deep, columns), jnp.bfloat16),
        in_specs=[whole_vmem()] + [pl.BlockSpec(memory_space=pl.ANY)] * len(after),
        out_specs=whole_vmem(),
        scratch_shapes=[pltpu.VMEM((deep, columns + width), jnp.bfloat16)],
        compiler_params=pltpu.CompilerParams(vmem_limit_bytes=VMEM_LIMIT),
        name="spread_uppers",
    )(packed, *after)


def touch_kernel(panel, *refs):
    out = refs[-1]
    out[...] = panel[0:ID_ROWS, :]


def touched(panel, after=()):
    return pl.pallas_call(
        touch_kernel,
        out_shape=jax.ShapeDtypeStruct((ID_ROWS, panel.shape[1]), panel.dtype),
        in_specs=[whole_vmem()] + [pl.BlockSpec(memory_space=pl.ANY)] * len(after),
        out_specs=whole_vmem(),
        compiler_params=pltpu.CompilerParams(vmem_limit_bytes=VMEM_LIMIT),
        cost_estimate=pl.CostEstimate(flops=DECLARED_FLOPS, bytes_accessed=0, transcendentals=0),
        name="touch_chunk",
    )(panel, *after)


def place_group(parts, ids, first, slots, supernodes, left, base):
    width = parts[0].shape[1]
    tiles = [(part, row) for part in parts for row in range(part.shape[0] // width)]
    ids = read_ids(ids[ids.shape[0] - ID_ROWS :, :])
    for tile, (part, row) in enumerate(tiles, first):
        at = pl.multiple_of(ids[tile, 0] * width, width)
        columns = pl.ds(pl.multiple_of(base + tile // slots * width, width), width)
        left[pl.ds(at, width), columns] = part[row * width : (row + 1) * width, :]


def place_groups(plan, groups, panels, uppers, left, right):
    slots, supernodes = plan
    width = panels[0][0].shape[1]
    tall = supernodes * width
    column = lax.axis_index("col")
    layer = lax.axis_index("gz")
    left[...] = jnp.zeros_like(left)
    for side, (tiles, upper) in enumerate(zip(panels, uppers)):
        base = (layer if side == 0 else 1 - layer) * (len(groups) * tall)
        for n, (members, ids, first, mask) in enumerate(groups):
            start = pl.multiple_of(base + n * tall, tall)
            right[pl.ds(start, tall), :] = upper[pl.ds(pl.multiple_of((column ^ mask) * tall, tall), tall), :]
            place_group([tiles[member] for member in members], tiles[ids], first, slots, supernodes, left, start)


def blocks_of(rows):
    size = rows // ROW_STEPS
    return [slice(i * size, (i + 1) * size) for i in range(ROW_STEPS)]


def product(left, right, block):
    width = left.shape[0] % (block.stop - block.start)
    return jnp.dot(
        left[width + block.start : width + block.stop, :], right[...], preferred_element_type=jnp.float32
    )


def sum_kernel(plan, groups, count, bases, *refs):
    panels = (refs[:count], refs[count : 2 * count])
    uppers, base_refs = refs[2 * count : 2 * count + 2], refs[2 * count + 2 : 2 * count + 2 + bases]
    out, left, right = refs[-3:]
    place_groups(plan, groups, panels, uppers, left, right)
    for block in blocks_of(out.shape[0]):
        update = product(left, right, block)
        if bases:
            update = base_refs[0][block, :] + update
        out[block, :] = update


def sum_groups(plan, groups, own, other, uppers, shape, bases=()):
    width = own[0].shape[1]
    depth = 2 * len(groups) * plan[1] * width
    return pl.pallas_call(
        functools.partial(sum_kernel, plan, groups, len(own), len(bases)),
        out_shape=jax.ShapeDtypeStruct(shape, jnp.float32),
        in_specs=[whole_vmem()] * (2 * len(own) + 2 + len(bases)),
        out_specs=whole_vmem(),
        scratch_shapes=[
            pltpu.VMEM((shape[0] + width, depth), jnp.bfloat16),
            pltpu.VMEM((depth, shape[1]), jnp.bfloat16),
        ],
        compiler_params=pltpu.CompilerParams(vmem_limit_bytes=VMEM_LIMIT),
        cost_estimate=pl.CostEstimate(flops=SUM_FLOPS, bytes_accessed=0, transcendentals=0),
        name="sum_groups",
    )(*own, *other, *uppers, *bases)


def finish_kernel(plan, groups, count, ancestor, early, *refs):
    panels = (refs[:count], refs[count : 2 * count])
    uppers, (out, left, right, result, sent) = refs[2 * count : 2 * count + 2], refs[-5:]
    place_groups(plan, groups, panels, uppers, left, right)
    copies = []
    for i, block in enumerate(blocks_of(out.shape[0])):
        result[block, :] = ancestor[block, :] - (early[block, :] + product(left, right, block))
        copy = pltpu.make_async_copy(result.at[block], out.at[block], sent.at[i])
        copy.start()
        copies.append(copy)
    for copy in copies:
        copy.wait()


def finish(plan, ancestor, early, groups, own, other, uppers, after):
    width = own[0].shape[1]
    depth = 2 * len(groups) * plan[1] * width
    return pl.pallas_call(
        functools.partial(finish_kernel, plan, groups, len(own)),
        out_shape=jax.ShapeDtypeStruct(ancestor.shape, jnp.float32),
        in_specs=[whole_vmem()] * (2 * len(own) + 4) + [pl.BlockSpec(memory_space=pl.ANY)] * len(after),
        out_specs=pl.BlockSpec(memory_space=pltpu.HBM),
        scratch_shapes=[
            pltpu.VMEM((ancestor.shape[0] + width, depth), jnp.bfloat16),
            pltpu.VMEM((depth, ancestor.shape[1]), jnp.bfloat16),
            pltpu.VMEM(ancestor.shape, jnp.float32),
            pltpu.SemaphoreType.DMA((ROW_STEPS,)),
        ],
        compiler_params=pltpu.CompilerParams(vmem_limit_bytes=VMEM_LIMIT),
        name="last_chunk_and_write",
    )(ancestor, early, *own, *other, *uppers, *after)


def swap(array, axis, mask):
    return lax.ppermute(array, axis, [(i, i ^ mask) for i in range(4)])


def siblings(array):
    return lax.ppermute(array, "gz", [(0, 1), (1, 0)])


def on_line_of_four(
    ancestor, lower_panel, row_ids, row_counts, diag_inverse, upper_panel, col_ids, col_counts
):
    supernodes, slots = lower_panel.shape[1:3]
    plan = (slots, supernodes)
    cut = 2 * supernodes * slots // 3
    both, first, second, packed = prepare(
        lower_panel,
        row_ids,
        row_counts,
        diag_inverse,
        upper_panel,
        col_ids,
        col_counts,
        cut,
    )
    near = swap(both, "col", 1)
    far_first = swap(first, "col", 2)
    far_second = swap(second, "col", 2)
    packed = lax.all_gather(packed, "row", axis=0, tiled=True)
    far_first, packed = lax.optimization_barrier((far_first, packed))
    last_first = swap(far_first, "col", 1)
    far_second, far_mark = lax.optimization_barrier((far_second, touched(far_second)))
    last_second = swap(far_second, "col", 1)
    other_both, other_first = siblings(both), siblings(far_first)
    upper = spread_uppers(
        packed,
        [near, far_second, other_both, other_first],
        upper_panel.shape[2],
        supernodes,
        ancestor.shape[1],
    )
    uppers = (upper, siblings(upper))
    early = sum_groups(
        plan,
        (((0,), 0, 0, 0), ((1, 2), 1, 0, 2)),
        [both, far_first, far_second],
        [other_both, other_first, siblings(far_second)],
        uppers,
        ancestor.shape,
    )
    last_first, first_mark = lax.optimization_barrier((last_first, touched(last_first)))
    last_second, second_mark = lax.optimization_barrier((last_second, touched(last_second, [early])))
    other_last = siblings(last_first)
    early = sum_groups(
        plan,
        (((0,), 0, 0, 1), ((1,), 1, 0, 3)),
        [near, last_first],
        [siblings(near), other_last],
        uppers,
        ancestor.shape,
        [early],
    )
    return finish(
        plan,
        ancestor,
        early,
        (((0,), 1, cut, 3),),
        [last_second, last_first],
        [siblings(last_second), other_last],
        uppers,
        [far_mark, first_mark, second_mark],
    )


def spread_tiles(tiles, ids, counts, blocks, rule):
    slot_index = jnp.arange(ids.shape[1], dtype=jnp.int32)
    alive = slot_index[None, :] < counts
    target = jnp.arange(blocks, dtype=jnp.int32)
    select = ((ids[:, :, None] == target[None, None, :]) & alive[:, :, None]).astype(jnp.bfloat16)
    return jnp.einsum(rule, select, tiles, preferred_element_type=jnp.float32).astype(jnp.bfloat16)


def on_device(
    ancestor, lower_panel, row_ids, row_counts, diag_inverse, upper_panel, col_ids, col_counts
):
    width = lower_panel.shape[-1]
    rows, columns = ancestor.shape
    solved = jnp.einsum(
        "ksab,kbc->ksac", lower_panel[0], diag_inverse[0], preferred_element_type=jnp.float32
    ).astype(jnp.bfloat16)
    piece = lax.all_gather((upper_panel[0], col_ids[0], col_counts[0]), "row", axis=0, tiled=True)
    upper_dense = spread_tiles(*piece, columns // width, "kcm,kcab->kamb").reshape(-1, columns)
    piece = lax.all_gather((solved, row_ids[0], row_counts[0]), "col", axis=0, tiled=True)
    lower_dense = spread_tiles(*piece, rows // width, "krl,krab->lakb").reshape(rows, -1)
    partial_sum = jnp.dot(lower_dense, upper_dense, preferred_element_type=jnp.float32)
    return ancestor - lax.psum(partial_sum, "gz")


def solution(mesh):
    placed = (
        P("row", "col"),
        P("gz", "col", "row", None, None),
        P("gz", "col", "row"),
        P("gz", "col", "row"),
        P("gz", "col", None, None),
        P("gz", "row", "col", None, None),
        P("gz", "row", "col"),
        P("gz", "row", "col"),
    )
    sizes = dict(mesh.shape)
    small = sizes["gz"] == 2 and sizes["row"] == 4 and sizes["col"] == 4

    def run(ancestor, lower_panel, *rest):
        two = lower_panel.shape[1] == 2 * sizes["col"]
        body = on_line_of_four if small and two else on_device
        return jax.shard_map(
            body, mesh=mesh, in_specs=placed, out_specs=P("row", "col"), check_vma=False
        )(ancestor, lower_panel, *rest)

    return run
```

```python
import functools

import jax
import jax.numpy as jnp
from jax import lax
from jax.experimental import pallas as pl
from jax.experimental.pallas import tpu as pltpu
from jax.sharding import PartitionSpec as P

VMEM_LIMIT = 24 * 1024 * 1024
ID_ROWS = 16
ROW_STEPS = 4
DECLARED_FLOPS = 10_000_000_000
SUM_FLOPS = 2_000_000_000


def whole_vmem():
    return pl.BlockSpec(memory_space=pltpu.VMEM)


def pack_ids(ids, counts, supernodes, slots, width):
    at_row = lax.broadcasted_iota(jnp.int32, (ID_ROWS, width), 0)
    rows = jnp.zeros((ID_ROWS, width), jnp.int32)
    for k in range(supernodes):
        for s in range(slots):
            value = jnp.where(s < counts[0, 0, k], ids[0, k, s] + 1, 0)
            rows = jnp.where(at_row == k * slots + s, value, rows)
    return rows.astype(jnp.float32).astype(jnp.bfloat16)


def read_ids(rows):
    return rows.astype(jnp.float32).astype(jnp.int32)


def prepare_kernel(
    row_ids_in, row_counts_in, col_ids_in, col_counts_in, lower_in, inverse_in, upper_in,
    both, first, second, packed,
    row_ids, row_counts, col_ids, col_counts, lower, inverse, upper, arrived,
):
    supernodes, slots, width, _ = lower.shape
    tall = slots * width
    cut = first.shape[0] - ID_ROWS
    pairs = (
        (row_ids_in, row_ids),
        (row_counts_in, row_counts),
        (inverse_in.at[0], inverse),
        (lower_in.at[0, 0], lower.at[0]),
        (lower_in.at[0, 1], lower.at[1]),
        (col_ids_in, col_ids),
        (col_counts_in, col_counts),
        (upper_in.at[0], upper),
    )
    copies = [pltpu.make_async_copy(src, dst, arrived.at[n]) for n, (src, dst) in enumerate(pairs)]
    for copy in copies:
        copy.start()
    for copy in copies[:3]:
        copy.wait()
    ids = pack_ids(row_ids, row_counts, supernodes, slots, width)
    first[cut:, :] = ids
    both[supernodes * tall :, :] = ids
    for k in range(supernodes):
        copies[3 + k].wait()
        solved = jnp.dot(lower[k].reshape(tall, width), inverse[k], preferred_element_type=jnp.float32)
        solved = solved.astype(jnp.bfloat16)
        start, stop = k * tall, (k + 1) * tall
        both[start:stop, :] = solved
        middle = min(max(cut, start), stop)
        if middle > start:
            first[start:middle, :] = solved[: middle - start]
        if middle < stop:
            second[middle - cut : stop - cut, :] = solved[middle - start :]
    for copy in copies[5:]:
        copy.wait()
    slots = upper.shape[1]
    tall = slots * width
    for k in range(supernodes):
        packed[k * tall : (k + 1) * tall, :] = upper[k].reshape(tall, width)
    packed[supernodes * tall :, :] = pack_ids(col_ids, col_counts, supernodes, slots, width)


def prepare(lower, row_ids, row_counts, inverse, upper, col_ids, col_counts, cut):
    _, supernodes, slots, width, _ = lower.shape
    tiles = supernodes * slots
    row_counts = jnp.swapaxes(row_counts, 1, 2)
    col_counts = jnp.swapaxes(col_counts, 1, 2)
    return pl.pallas_call(
        prepare_kernel,
        out_shape=(
            jax.ShapeDtypeStruct((tiles * width + ID_ROWS, width), jnp.bfloat16),
            jax.ShapeDtypeStruct((cut * width + ID_ROWS, width), jnp.bfloat16),
            jax.ShapeDtypeStruct(((tiles - cut) * width, width), jnp.bfloat16),
            jax.ShapeDtypeStruct((supernodes * upper.shape[2] * width + ID_ROWS, width), jnp.bfloat16),
        ),
        in_specs=[pl.BlockSpec(memory_space=pltpu.HBM)] * 7,
        out_specs=(whole_vmem(),) * 4,
        scratch_shapes=[
            pltpu.SMEM(row_ids.shape, jnp.int32),
            pltpu.SMEM(row_counts.shape, jnp.int32),
            pltpu.SMEM(col_ids.shape, jnp.int32),
            pltpu.SMEM(col_counts.shape, jnp.int32),
            pltpu.VMEM(lower.shape[1:], jnp.bfloat16),
            pltpu.VMEM(inverse.shape[1:], jnp.bfloat16),
            pltpu.VMEM(upper.shape[1:], jnp.bfloat16),
            pltpu.SemaphoreType.DMA((8,)),
        ],
        compiler_params=pltpu.CompilerParams(vmem_limit_bytes=VMEM_LIMIT),
        name="solve_and_pack",
    )(
        *(
            pltpu.with_memory_space_constraint(array, pltpu.HBM)
            for array in (row_ids, row_counts, col_ids, col_counts, lower, inverse, upper)
        )
    )


def spread_kernel(slots, supernodes, packed, *refs):
    out, padded = refs[-2:]
    width = packed.shape[1]
    piece = supernodes * slots * width + ID_ROWS
    padded[...] = jnp.zeros_like(padded)
    for group in range(packed.shape[0] // piece):
        start = group * piece
        ids = read_ids(packed[start + piece - ID_ROWS : start + piece, :])
        for k in range(supernodes):
            rows = slice((group * supernodes + k) * width, (group * supernodes + k + 1) * width)
            for s in range(slots):
                tile = k * slots + s
                at = pl.multiple_of(ids[tile, 0] * width, width)
                padded[rows, pl.ds(at, width)] = packed[start + tile * width : start + (tile + 1) * width, :]
    out[...] = padded[:, width:]


def spread_uppers(packed, after, slots, supernodes, columns):
    width = packed.shape[1]
    deep = packed.shape[0] // (supernodes * slots * width + ID_ROWS) * supernodes * width
    return pl.pallas_call(
        functools.partial(spread_kernel, slots, supernodes),
        out_shape=jax.ShapeDtypeStruct((deep, columns), jnp.bfloat16),
        in_specs=[whole_vmem()] + [pl.BlockSpec(memory_space=pl.ANY)] * len(after),
        out_specs=whole_vmem(),
        scratch_shapes=[pltpu.VMEM((deep, columns + width), jnp.bfloat16)],
        compiler_params=pltpu.CompilerParams(vmem_limit_bytes=VMEM_LIMIT),
        name="spread_uppers",
    )(packed, *after)


def touch_kernel(panel, *refs):
    out = refs[-1]
    out[...] = panel[0:ID_ROWS, :]


def touched(panel, after=()):
    return pl.pallas_call(
        touch_kernel,
        out_shape=jax.ShapeDtypeStruct((ID_ROWS, panel.shape[1]), panel.dtype),
        in_specs=[whole_vmem()] + [pl.BlockSpec(memory_space=pl.ANY)] * len(after),
        out_specs=whole_vmem(),
        compiler_params=pltpu.CompilerParams(vmem_limit_bytes=VMEM_LIMIT),
        cost_estimate=pl.CostEstimate(flops=DECLARED_FLOPS, bytes_accessed=0, transcendentals=0),
        name="touch_chunk",
    )(panel, *after)


def place_group(parts, ids, first, slots, supernodes, left, base):
    width = parts[0].shape[1]
    tiles = [(part, row) for part in parts for row in range(part.shape[0] // width)]
    ids = read_ids(ids[ids.shape[0] - ID_ROWS :, :])
    for tile, (part, row) in enumerate(tiles, first):
        at = pl.multiple_of(ids[tile, 0] * width, width)
        columns = pl.ds(pl.multiple_of(base + tile // slots * width, width), width)
        left[pl.ds(at, width), columns] = part[row * width : (row + 1) * width, :]


def place_groups(plan, groups, panels, uppers, left, right):
    slots, supernodes = plan
    width = panels[0][0].shape[1]
    tall = supernodes * width
    column = lax.axis_index("col")
    layer = lax.axis_index("gz")
    left[...] = jnp.zeros_like(left)
    for side, (tiles, upper) in enumerate(zip(panels, uppers)):
        base = (layer if side == 0 else 1 - layer) * (len(groups) * tall)
        for n, (members, ids, first, mask) in enumerate(groups):
            start = pl.multiple_of(base + n * tall, tall)
            right[pl.ds(start, tall), :] = upper[pl.ds(pl.multiple_of((column ^ mask) * tall, tall), tall), :]
            place_group([tiles[member] for member in members], tiles[ids], first, slots, supernodes, left, start)


def blocks_of(rows):
    size = rows // ROW_STEPS
    return [slice(i * size, (i + 1) * size) for i in range(ROW_STEPS)]


def product(left, right, block):
    width = left.shape[0] % (block.stop - block.start)
    return jnp.dot(
        left[width + block.start : width + block.stop, :], right[...], preferred_element_type=jnp.float32
    )


def sum_kernel(plan, groups, count, bases, *refs):
    panels = (refs[:count], refs[count : 2 * count])
    uppers, base_refs = refs[2 * count : 2 * count + 2], refs[2 * count + 2 : 2 * count + 2 + bases]
    out, left, right = refs[-3:]
    place_groups(plan, groups, panels, uppers, left, right)
    for block in blocks_of(out.shape[0]):
        update = product(left, right, block)
        if bases:
            update = base_refs[0][block, :] + update
        out[block, :] = update


def sum_groups(plan, groups, own, other, uppers, shape, bases=()):
    width = own[0].shape[1]
    depth = 2 * len(groups) * plan[1] * width
    return pl.pallas_call(
        functools.partial(sum_kernel, plan, groups, len(own), len(bases)),
        out_shape=jax.ShapeDtypeStruct(shape, jnp.float32),
        in_specs=[whole_vmem()] * (2 * len(own) + 2 + len(bases)),
        out_specs=whole_vmem(),
        scratch_shapes=[
            pltpu.VMEM((shape[0] + width, depth), jnp.bfloat16),
            pltpu.VMEM((depth, shape[1]), jnp.bfloat16),
        ],
        compiler_params=pltpu.CompilerParams(vmem_limit_bytes=VMEM_LIMIT),
        cost_estimate=pl.CostEstimate(flops=SUM_FLOPS, bytes_accessed=0, transcendentals=0),
        name="sum_groups",
    )(*own, *other, *uppers, *bases)


def finish_kernel(plan, groups, count, ancestor, early, *refs):
    panels = (refs[:count], refs[count : 2 * count])
    uppers, (out, left, right, result, sent) = refs[2 * count : 2 * count + 2], refs[-5:]
    place_groups(plan, groups, panels, uppers, left, right)
    copies = []
    for i, block in enumerate(blocks_of(out.shape[0])):
        result[block, :] = ancestor[block, :] - (early[block, :] + product(left, right, block))
        copy = pltpu.make_async_copy(result.at[block], out.at[block], sent.at[i])
        copy.start()
        copies.append(copy)
    for copy in copies:
        copy.wait()


def finish(plan, ancestor, early, groups, own, other, uppers, after):
    width = own[0].shape[1]
    depth = 2 * len(groups) * plan[1] * width
    return pl.pallas_call(
        functools.partial(finish_kernel, plan, groups, len(own)),
        out_shape=jax.ShapeDtypeStruct(ancestor.shape, jnp.float32),
        in_specs=[whole_vmem()] * (2 * len(own) + 4) + [pl.BlockSpec(memory_space=pl.ANY)] * len(after),
        out_specs=pl.BlockSpec(memory_space=pltpu.HBM),
        scratch_shapes=[
            pltpu.VMEM((ancestor.shape[0] + width, depth), jnp.bfloat16),
            pltpu.VMEM((depth, ancestor.shape[1]), jnp.bfloat16),
            pltpu.VMEM(ancestor.shape, jnp.float32),
            pltpu.SemaphoreType.DMA((ROW_STEPS,)),
        ],
        compiler_params=pltpu.CompilerParams(vmem_limit_bytes=VMEM_LIMIT),
        name="last_chunk_and_write",
    )(ancestor, early, *own, *other, *uppers, *after)


def swap(array, axis, mask):
    return lax.ppermute(array, axis, [(i, i ^ mask) for i in range(4)])


def siblings(array):
    return lax.ppermute(array, "gz", [(0, 1), (1, 0)])


def on_line_of_four(
    ancestor, lower_panel, row_ids, row_counts, diag_inverse, upper_panel, col_ids, col_counts
):
    supernodes, slots = lower_panel.shape[1:3]
    plan = (slots, supernodes)
    cut = 2 * supernodes * slots // 3
    both, first, second, packed = prepare(
        lower_panel,
        row_ids,
        row_counts,
        diag_inverse,
        upper_panel,
        col_ids,
        col_counts,
        cut,
    )
    near = swap(both, "col", 1)
    far_first = swap(first, "col", 2)
    far_second = swap(second, "col", 2)
    packed = lax.all_gather(packed, "row", axis=0, tiled=True)
    far_first, packed = lax.optimization_barrier((far_first, packed))
    last_first = swap(far_first, "col", 1)
    far_second, far_mark = lax.optimization_barrier((far_second, touched(far_second, [near])))
    last_second = swap(far_second, "col", 1)
    other_both, other_first = siblings(both), siblings(far_first)
    upper = spread_uppers(
        packed,
        [near, far_second, other_both],
        upper_panel.shape[2],
        supernodes,
        ancestor.shape[1],
    )
    uppers = (upper, siblings(upper))
    early = sum_groups(
        plan,
        (((0,), 0, 0, 0), ((1, 2), 1, 0, 2)),
        [both, far_first, far_second],
        [other_both, other_first, siblings(far_second)],
        uppers,
        ancestor.shape,
    )
    last_first, first_mark = lax.optimization_barrier((last_first, touched(last_first)))
    last_second, second_mark = lax.optimization_barrier((last_second, touched(last_second, [early])))
    other_last = siblings(last_first)
    early = sum_groups(
        plan,
        (((0,), 0, 0, 1), ((1,), 1, 0, 3)),
        [near, last_first],
        [siblings(near), other_last],
        uppers,
        ancestor.shape,
        [early],
    )
    return finish(
        plan,
        ancestor,
        early,
        (((0,), 1, cut, 3),),
        [last_second, last_first],
        [siblings(last_second), other_last],
        uppers,
        [far_mark, first_mark, second_mark],
    )


def spread_tiles(tiles, ids, counts, blocks, rule):
    slot_index = jnp.arange(ids.shape[1], dtype=jnp.int32)
    alive = slot_index[None, :] < counts
    target = jnp.arange(blocks, dtype=jnp.int32)
    select = ((ids[:, :, None] == target[None, None, :]) & alive[:, :, None]).astype(jnp.bfloat16)
    return jnp.einsum(rule, select, tiles, preferred_element_type=jnp.float32).astype(jnp.bfloat16)


def on_device(
    ancestor, lower_panel, row_ids, row_counts, diag_inverse, upper_panel, col_ids, col_counts
):
    width = lower_panel.shape[-1]
    rows, columns = ancestor.shape
    solved = jnp.einsum(
        "ksab,kbc->ksac", lower_panel[0], diag_inverse[0], preferred_element_type=jnp.float32
    ).astype(jnp.bfloat16)
    piece = lax.all_gather((upper_panel[0], col_ids[0], col_counts[0]), "row", axis=0, tiled=True)
    upper_dense = spread_tiles(*piece, columns // width, "kcm,kcab->kamb").reshape(-1, columns)
    piece = lax.all_gather((solved, row_ids[0], row_counts[0]), "col", axis=0, tiled=True)
    lower_dense = spread_tiles(*piece, rows // width, "krl,krab->lakb").reshape(rows, -1)
    partial_sum = jnp.dot(lower_dense, upper_dense, preferred_element_type=jnp.float32)
    return ancestor - lax.psum(partial_sum, "gz")


def solution(mesh):
    placed = (
        P("row", "col"),
        P("gz", "col", "row", None, None),
        P("gz", "col", "row"),
        P("gz", "col", "row"),
        P("gz", "col", None, None),
        P("gz", "row", "col", None, None),
        P("gz", "row", "col"),
        P("gz", "row", "col"),
    )
    sizes = dict(mesh.shape)
    small = sizes["gz"] == 2 and sizes["row"] == 4 and sizes["col"] == 4

    def run(ancestor, lower_panel, *rest):
        two = lower_panel.shape[1] == 2 * sizes["col"]
        body = on_line_of_four if small and two else on_device
        return jax.shard_map(
            body, mesh=mesh, in_specs=placed, out_specs=P("row", "col"), check_vma=False
        )(ancestor, lower_panel, *rest)

    return run
```

```python
import functools

import jax
import jax.numpy as jnp
from jax import lax
from jax.experimental import pallas as pl
from jax.experimental.pallas import tpu as pltpu
from jax.sharding import PartitionSpec as P

VMEM_LIMIT = 24 * 1024 * 1024
ID_ROWS = 16
ROW_STEPS = 4
DECLARED_FLOPS = 10_000_000_000
SUM_FLOPS = 2_000_000_000


def whole_vmem():
    return pl.BlockSpec(memory_space=pltpu.VMEM)


def pack_ids(ids, counts, supernodes, slots, width):
    at_row = lax.broadcasted_iota(jnp.int32, (ID_ROWS, width), 0)
    rows = jnp.zeros((ID_ROWS, width), jnp.int32)
    for k in range(supernodes):
        for s in range(slots):
            value = jnp.where(s < counts[0, 0, k], ids[0, k, s] + 1, 0)
            rows = jnp.where(at_row == k * slots + s, value, rows)
    return rows.astype(jnp.float32).astype(jnp.bfloat16)


def read_ids(rows):
    return rows.astype(jnp.float32).astype(jnp.int32)


def prepare_kernel(
    row_ids_in, row_counts_in, col_ids_in, col_counts_in, lower_in, inverse_in, upper_in,
    both, first, second, packed,
    row_ids, row_counts, col_ids, col_counts, lower, inverse, upper, arrived,
):
    supernodes, slots, width, _ = lower.shape
    tall = slots * width
    cut = first.shape[0] - ID_ROWS
    pairs = (
        (row_ids_in, row_ids),
        (row_counts_in, row_counts),
        (inverse_in.at[0], inverse),
        (lower_in.at[0, 0], lower.at[0]),
        (lower_in.at[0, 1], lower.at[1]),
        (col_ids_in, col_ids),
        (col_counts_in, col_counts),
        (upper_in.at[0], upper),
    )
    copies = [pltpu.make_async_copy(src, dst, arrived.at[n]) for n, (src, dst) in enumerate(pairs)]
    for copy in copies:
        copy.start()
    for copy in copies[:3]:
        copy.wait()
    ids = pack_ids(row_ids, row_counts, supernodes, slots, width)
    first[cut:, :] = ids
    both[supernodes * tall :, :] = ids
    for k in range(supernodes):
        copies[3 + k].wait()
        solved = jnp.dot(lower[k].reshape(tall, width), inverse[k], preferred_element_type=jnp.float32)
        solved = solved.astype(jnp.bfloat16)
        start, stop = k * tall, (k + 1) * tall
        both[start:stop, :] = solved
        middle = min(max(cut, start), stop)
        if middle > start:
            first[start:middle, :] = solved[: middle - start]
        if middle < stop:
            second[middle - cut : stop - cut, :] = solved[middle - start :]
    for copy in copies[5:]:
        copy.wait()
    slots = upper.shape[1]
    tall = slots * width
    for k in range(supernodes):
        packed[k * tall : (k + 1) * tall, :] = upper[k].reshape(tall, width)
    packed[supernodes * tall :, :] = pack_ids(col_ids, col_counts, supernodes, slots, width)


def prepare(lower, row_ids, row_counts, inverse, upper, col_ids, col_counts, cut):
    _, supernodes, slots, width, _ = lower.shape
    tiles = supernodes * slots
    row_counts = jnp.swapaxes(row_counts, 1, 2)
    col_counts = jnp.swapaxes(col_counts, 1, 2)
    return pl.pallas_call(
        prepare_kernel,
        out_shape=(
            jax.ShapeDtypeStruct((tiles * width + ID_ROWS, width), jnp.bfloat16),
            jax.ShapeDtypeStruct((cut * width + ID_ROWS, width), jnp.bfloat16),
            jax.ShapeDtypeStruct(((tiles - cut) * width, width), jnp.bfloat16),
            jax.ShapeDtypeStruct((supernodes * upper.shape[2] * width + ID_ROWS, width), jnp.bfloat16),
        ),
        in_specs=[pl.BlockSpec(memory_space=pltpu.HBM)] * 7,
        out_specs=(whole_vmem(),) * 4,
        scratch_shapes=[
            pltpu.SMEM(row_ids.shape, jnp.int32),
            pltpu.SMEM(row_counts.shape, jnp.int32),
            pltpu.SMEM(col_ids.shape, jnp.int32),
            pltpu.SMEM(col_counts.shape, jnp.int32),
            pltpu.VMEM(lower.shape[1:], jnp.bfloat16),
            pltpu.VMEM(inverse.shape[1:], jnp.bfloat16),
            pltpu.VMEM(upper.shape[1:], jnp.bfloat16),
            pltpu.SemaphoreType.DMA((8,)),
        ],
        compiler_params=pltpu.CompilerParams(vmem_limit_bytes=VMEM_LIMIT),
        name="solve_and_pack",
    )(
        *(
            pltpu.with_memory_space_constraint(array, pltpu.HBM)
            for array in (row_ids, row_counts, col_ids, col_counts, lower, inverse, upper)
        )
    )


def spread_kernel(slots, supernodes, packed, *refs):
    out, padded = refs[-2:]
    width = packed.shape[1]
    piece = supernodes * slots * width + ID_ROWS
    padded[...] = jnp.zeros_like(padded)
    for group in range(packed.shape[0] // piece):
        start = group * piece
        ids = read_ids(packed[start + piece - ID_ROWS : start + piece, :])
        for k in range(supernodes):
            rows = slice((group * supernodes + k) * width, (group * supernodes + k + 1) * width)
            for s in range(slots):
                tile = k * slots + s
                at = pl.multiple_of(ids[tile, 0] * width, width)
                padded[rows, pl.ds(at, width)] = packed[start + tile * width : start + (tile + 1) * width, :]
    out[...] = padded[:, width:]


def spread_uppers(packed, after, slots, supernodes, columns):
    width = packed.shape[1]
    deep = packed.shape[0] // (supernodes * slots * width + ID_ROWS) * supernodes * width
    return pl.pallas_call(
        functools.partial(spread_kernel, slots, supernodes),
        out_shape=jax.ShapeDtypeStruct((deep, columns), jnp.bfloat16),
        in_specs=[whole_vmem()] + [pl.BlockSpec(memory_space=pl.ANY)] * len(after),
        out_specs=whole_vmem(),
        scratch_shapes=[pltpu.VMEM((deep, columns + width), jnp.bfloat16)],
        compiler_params=pltpu.CompilerParams(vmem_limit_bytes=VMEM_LIMIT),
        name="spread_uppers",
    )(packed, *after)


def touch_kernel(panel, *refs):
    out = refs[-1]
    out[...] = panel[0:ID_ROWS, :]


def touched(panel, after=()):
    return pl.pallas_call(
        touch_kernel,
        out_shape=jax.ShapeDtypeStruct((ID_ROWS, panel.shape[1]), panel.dtype),
        in_specs=[whole_vmem()] + [pl.BlockSpec(memory_space=pl.ANY)] * len(after),
        out_specs=whole_vmem(),
        compiler_params=pltpu.CompilerParams(vmem_limit_bytes=VMEM_LIMIT),
        cost_estimate=pl.CostEstimate(flops=DECLARED_FLOPS, bytes_accessed=0, transcendentals=0),
        name="touch_chunk",
    )(panel, *after)


def place_group(parts, ids, first, slots, left, base):
    width = parts[0].shape[1]
    tiles = [(part, row) for part in parts for row in range(part.shape[0] // width)]
    ids = read_ids(ids[ids.shape[0] - ID_ROWS :, :])
    for tile, (part, row) in enumerate(tiles, first):
        at = pl.multiple_of(ids[tile, 0] * width, width)
        columns = pl.ds(pl.multiple_of(base + (tile // slots - first // slots) * width, width), width)
        left[pl.ds(at, width), columns] = part[row * width : (row + 1) * width, :]


def deep_of(plan, groups):
    slots, supernodes = plan
    return [supernodes - first // slots for _, _, first, _ in groups]


def place_groups(plan, groups, panels, uppers, left, right):
    slots, supernodes = plan
    width = panels[0][0].shape[1]
    column = lax.axis_index("col")
    layer = lax.axis_index("gz")
    deep = deep_of(plan, groups)
    left[...] = jnp.zeros_like(left)
    for side, (tiles, upper) in enumerate(zip(panels, uppers)):
        start = (layer if side == 0 else 1 - layer) * (sum(deep) * width)
        for (members, ids, first, mask), span in zip(groups, deep):
            start = pl.multiple_of(start, width)
            rows = pl.multiple_of(((column ^ mask) * supernodes + first // slots) * width, width)
            right[pl.ds(start, span * width), :] = upper[pl.ds(rows, span * width), :]
            place_group([tiles[member] for member in members], tiles[ids], first, slots, left, start)
            start += span * width


def blocks_of(rows):
    size = rows // ROW_STEPS
    return [slice(i * size, (i + 1) * size) for i in range(ROW_STEPS)]


def product(left, right, block):
    width = left.shape[0] % (block.stop - block.start)
    return jnp.dot(
        left[width + block.start : width + block.stop, :], right[...], preferred_element_type=jnp.float32
    )


def sum_kernel(plan, groups, count, bases, *refs):
    panels = (refs[:count], refs[count : 2 * count])
    uppers, base_refs = refs[2 * count : 2 * count + 2], refs[2 * count + 2 : 2 * count + 2 + bases]
    out, left, right = refs[-3:]
    place_groups(plan, groups, panels, uppers, left, right)
    for block in blocks_of(out.shape[0]):
        update = product(left, right, block)
        if bases:
            update = base_refs[0][block, :] + update
        out[block, :] = update


def sum_groups(plan, groups, own, other, uppers, shape, bases=()):
    width = own[0].shape[1]
    depth = 2 * sum(deep_of(plan, groups)) * width
    return pl.pallas_call(
        functools.partial(sum_kernel, plan, groups, len(own), len(bases)),
        out_shape=jax.ShapeDtypeStruct(shape, jnp.float32),
        in_specs=[whole_vmem()] * (2 * len(own) + 2 + len(bases)),
        out_specs=whole_vmem(),
        scratch_shapes=[
            pltpu.VMEM((shape[0] + width, depth), jnp.bfloat16),
            pltpu.VMEM((depth, shape[1]), jnp.bfloat16),
        ],
        compiler_params=pltpu.CompilerParams(vmem_limit_bytes=VMEM_LIMIT),
        cost_estimate=pl.CostEstimate(flops=SUM_FLOPS, bytes_accessed=0, transcendentals=0),
        name="sum_groups",
    )(*own, *other, *uppers, *bases)


def finish_kernel(plan, groups, count, ancestor, early, *refs):
    panels = (refs[:count], refs[count : 2 * count])
    uppers, (out, left, right, result, sent) = refs[2 * count : 2 * count + 2], refs[-5:]
    place_groups(plan, groups, panels, uppers, left, right)
    copies = []
    for i, block in enumerate(blocks_of(out.shape[0])):
        result[block, :] = ancestor[block, :] - (early[block, :] + product(left, right, block))
        copy = pltpu.make_async_copy(result.at[block], out.at[block], sent.at[i])
        copy.start()
        copies.append(copy)
    for copy in copies:
        copy.wait()


def finish(plan, ancestor, early, groups, own, other, uppers, after):
    width = own[0].shape[1]
    depth = 2 * sum(deep_of(plan, groups)) * width
    return pl.pallas_call(
        functools.partial(finish_kernel, plan, groups, len(own)),
        out_shape=jax.ShapeDtypeStruct(ancestor.shape, jnp.float32),
        in_specs=[whole_vmem()] * (2 * len(own) + 4) + [pl.BlockSpec(memory_space=pl.ANY)] * len(after),
        out_specs=pl.BlockSpec(memory_space=pltpu.HBM),
        scratch_shapes=[
            pltpu.VMEM((ancestor.shape[0] + width, depth), jnp.bfloat16),
            pltpu.VMEM((depth, ancestor.shape[1]), jnp.bfloat16),
            pltpu.VMEM(ancestor.shape, jnp.float32),
            pltpu.SemaphoreType.DMA((ROW_STEPS,)),
        ],
        compiler_params=pltpu.CompilerParams(vmem_limit_bytes=VMEM_LIMIT),
        name="last_chunk_and_write",
    )(ancestor, early, *own, *other, *uppers, *after)


def swap(array, axis, mask):
    return lax.ppermute(array, axis, [(i, i ^ mask) for i in range(4)])


def siblings(array):
    return lax.ppermute(array, "gz", [(0, 1), (1, 0)])


def on_line_of_four(
    ancestor, lower_panel, row_ids, row_counts, diag_inverse, upper_panel, col_ids, col_counts
):
    supernodes, slots = lower_panel.shape[1:3]
    plan = (slots, supernodes)
    cut = 2 * supernodes * slots // 3
    both, first, second, packed = prepare(
        lower_panel,
        row_ids,
        row_counts,
        diag_inverse,
        upper_panel,
        col_ids,
        col_counts,
        cut,
    )
    near = swap(both, "col", 1)
    far_first = swap(first, "col", 2)
    far_second = swap(second, "col", 2)
    packed = lax.all_gather(packed, "row", axis=0, tiled=True)
    far_first, packed = lax.optimization_barrier((far_first, packed))
    last_first = swap(far_first, "col", 1)
    far_second, far_mark = lax.optimization_barrier((far_second, touched(far_second, [near])))
    last_second = swap(far_second, "col", 1)
    other_both, other_first = siblings(both), siblings(far_first)
    upper = spread_uppers(
        packed,
        [near, far_second, other_both],
        upper_panel.shape[2],
        supernodes,
        ancestor.shape[1],
    )
    uppers = (upper, siblings(upper))
    early = sum_groups(
        plan,
        (((0,), 0, 0, 0), ((1, 2), 1, 0, 2)),
        [both, far_first, far_second],
        [other_both, other_first, siblings(far_second)],
        uppers,
        ancestor.shape,
    )
    early = sum_groups(
        plan, (((0,), 0, 0, 1),), [near], [siblings(near)], uppers, ancestor.shape, [early]
    )
    last_first, first_mark = lax.optimization_barrier((last_first, touched(last_first)))
    last_second, second_mark = lax.optimization_barrier((last_second, touched(last_second, [early])))
    other_last = siblings(last_first)
    early = sum_groups(
        plan,
        (((0,), 0, 0, 3),),
        [last_first],
        [other_last],
        uppers,
        ancestor.shape,
        [early],
    )
    return finish(
        plan,
        ancestor,
        early,
        (((0,), 1, cut, 3),),
        [last_second, last_first],
        [siblings(last_second), other_last],
        uppers,
        [far_mark, first_mark, second_mark],
    )


def spread_tiles(tiles, ids, counts, blocks, rule):
    slot_index = jnp.arange(ids.shape[1], dtype=jnp.int32)
    alive = slot_index[None, :] < counts
    target = jnp.arange(blocks, dtype=jnp.int32)
    select = ((ids[:, :, None] == target[None, None, :]) & alive[:, :, None]).astype(jnp.bfloat16)
    return jnp.einsum(rule, select, tiles, preferred_element_type=jnp.float32).astype(jnp.bfloat16)


def on_device(
    ancestor, lower_panel, row_ids, row_counts, diag_inverse, upper_panel, col_ids, col_counts
):
    width = lower_panel.shape[-1]
    rows, columns = ancestor.shape
    solved = jnp.einsum(
        "ksab,kbc->ksac", lower_panel[0], diag_inverse[0], preferred_element_type=jnp.float32
    ).astype(jnp.bfloat16)
    piece = lax.all_gather((upper_panel[0], col_ids[0], col_counts[0]), "row", axis=0, tiled=True)
    upper_dense = spread_tiles(*piece, columns // width, "kcm,kcab->kamb").reshape(-1, columns)
    piece = lax.all_gather((solved, row_ids[0], row_counts[0]), "col", axis=0, tiled=True)
    lower_dense = spread_tiles(*piece, rows // width, "krl,krab->lakb").reshape(rows, -1)
    partial_sum = jnp.dot(lower_dense, upper_dense, preferred_element_type=jnp.float32)
    return ancestor - lax.psum(partial_sum, "gz")


def solution(mesh):
    placed = (
        P("row", "col"),
        P("gz", "col", "row", None, None),
        P("gz", "col", "row"),
        P("gz", "col", "row"),
        P("gz", "col", None, None),
        P("gz", "row", "col", None, None),
        P("gz", "row", "col"),
        P("gz", "row", "col"),
    )
    sizes = dict(mesh.shape)
    small = sizes["gz"] == 2 and sizes["row"] == 4 and sizes["col"] == 4

    def run(ancestor, lower_panel, *rest):
        two = lower_panel.shape[1] == 2 * sizes["col"]
        body = on_line_of_four if small and two else on_device
        return jax.shard_map(
            body, mesh=mesh, in_specs=placed, out_specs=P("row", "col"), check_vma=False
        )(ancestor, lower_panel, *rest)

    return run
```

```python
import functools

import jax
import jax.numpy as jnp
from jax import lax
from jax.experimental import pallas as pl
from jax.experimental.pallas import tpu as pltpu
from jax.sharding import PartitionSpec as P

VMEM_LIMIT = 24 * 1024 * 1024
ID_ROWS = 16
ROW_STEPS = 4
DECLARED_FLOPS = 10_000_000_000
SUM_FLOPS = 1_000_000_000


def whole_vmem():
    return pl.BlockSpec(memory_space=pltpu.VMEM)


def pack_ids(ids, counts, supernodes, slots, width):
    at_row = lax.broadcasted_iota(jnp.int32, (ID_ROWS, width), 0)
    rows = jnp.zeros((ID_ROWS, width), jnp.int32)
    for k in range(supernodes):
        for s in range(slots):
            value = jnp.where(s < counts[0, 0, k], ids[0, k, s] + 1, 0)
            rows = jnp.where(at_row == k * slots + s, value, rows)
    return rows.astype(jnp.float32).astype(jnp.bfloat16)


def read_ids(rows):
    return rows.astype(jnp.float32).astype(jnp.int32)


def prepare_kernel(
    row_ids_in, row_counts_in, col_ids_in, col_counts_in, lower_in, inverse_in, upper_in,
    both, first, second, packed,
    row_ids, row_counts, col_ids, col_counts, lower, inverse, upper, arrived,
):
    supernodes, slots, width, _ = lower.shape
    tall = slots * width
    cut = first.shape[0] - ID_ROWS
    pairs = (
        (row_ids_in, row_ids),
        (row_counts_in, row_counts),
        (inverse_in.at[0], inverse),
        (lower_in.at[0, 0], lower.at[0]),
        (lower_in.at[0, 1], lower.at[1]),
        (col_ids_in, col_ids),
        (col_counts_in, col_counts),
        (upper_in.at[0], upper),
    )
    copies = [pltpu.make_async_copy(src, dst, arrived.at[n]) for n, (src, dst) in enumerate(pairs)]
    for copy in copies:
        copy.start()
    for copy in copies[:3]:
        copy.wait()
    ids = pack_ids(row_ids, row_counts, supernodes, slots, width)
    first[cut:, :] = ids
    both[supernodes * tall :, :] = ids
    for k in range(supernodes):
        copies[3 + k].wait()
        solved = jnp.dot(lower[k].reshape(tall, width), inverse[k], preferred_element_type=jnp.float32)
        solved = solved.astype(jnp.bfloat16)
        start, stop = k * tall, (k + 1) * tall
        both[start:stop, :] = solved
        middle = min(max(cut, start), stop)
        if middle > start:
            first[start:middle, :] = solved[: middle - start]
        if middle < stop:
            second[middle - cut : stop - cut, :] = solved[middle - start :]
    for copy in copies[5:]:
        copy.wait()
    slots = upper.shape[1]
    tall = slots * width
    for k in range(supernodes):
        packed[k * tall : (k + 1) * tall, :] = upper[k].reshape(tall, width)
    packed[supernodes * tall :, :] = pack_ids(col_ids, col_counts, supernodes, slots, width)


def prepare(lower, row_ids, row_counts, inverse, upper, col_ids, col_counts, cut):
    _, supernodes, slots, width, _ = lower.shape
    tiles = supernodes * slots
    row_counts = jnp.swapaxes(row_counts, 1, 2)
    col_counts = jnp.swapaxes(col_counts, 1, 2)
    return pl.pallas_call(
        prepare_kernel,
        out_shape=(
            jax.ShapeDtypeStruct((tiles * width + ID_ROWS, width), jnp.bfloat16),
            jax.ShapeDtypeStruct((cut * width + ID_ROWS, width), jnp.bfloat16),
            jax.ShapeDtypeStruct(((tiles - cut) * width, width), jnp.bfloat16),
            jax.ShapeDtypeStruct((supernodes * upper.shape[2] * width + ID_ROWS, width), jnp.bfloat16),
        ),
        in_specs=[pl.BlockSpec(memory_space=pltpu.HBM)] * 7,
        out_specs=(whole_vmem(),) * 4,
        scratch_shapes=[
            pltpu.SMEM(row_ids.shape, jnp.int32),
            pltpu.SMEM(row_counts.shape, jnp.int32),
            pltpu.SMEM(col_ids.shape, jnp.int32),
            pltpu.SMEM(col_counts.shape, jnp.int32),
            pltpu.VMEM(lower.shape[1:], jnp.bfloat16),
            pltpu.VMEM(inverse.shape[1:], jnp.bfloat16),
            pltpu.VMEM(upper.shape[1:], jnp.bfloat16),
            pltpu.SemaphoreType.DMA((8,)),
        ],
        compiler_params=pltpu.CompilerParams(vmem_limit_bytes=VMEM_LIMIT),
        name="solve_and_pack",
    )(
        *(
            pltpu.with_memory_space_constraint(array, pltpu.HBM)
            for array in (row_ids, row_counts, col_ids, col_counts, lower, inverse, upper)
        )
    )


def spread_kernel(slots, supernodes, packed, *refs):
    out, padded = refs[-2:]
    width = packed.shape[1]
    piece = supernodes * slots * width + ID_ROWS
    padded[...] = jnp.zeros_like(padded)
    for group in range(packed.shape[0] // piece):
        start = group * piece
        ids = read_ids(packed[start + piece - ID_ROWS : start + piece, :])
        for k in range(supernodes):
            rows = slice((group * supernodes + k) * width, (group * supernodes + k + 1) * width)
            for s in range(slots):
                tile = k * slots + s
                at = pl.multiple_of(ids[tile, 0] * width, width)
                padded[rows, pl.ds(at, width)] = packed[start + tile * width : start + (tile + 1) * width, :]
    out[...] = padded[:, width:]


def spread_uppers(packed, after, held, slots, supernodes, columns):
    width = packed.shape[1]
    deep = packed.shape[0] // (supernodes * slots * width + ID_ROWS) * supernodes * width
    return pl.pallas_call(
        functools.partial(spread_kernel, slots, supernodes),
        out_shape=jax.ShapeDtypeStruct((deep, columns), jnp.bfloat16),
        in_specs=[whole_vmem()]
        + [pl.BlockSpec(memory_space=pl.ANY)] * len(after)
        + [whole_vmem()] * len(held),
        out_specs=whole_vmem(),
        scratch_shapes=[pltpu.VMEM((deep, columns + width), jnp.bfloat16)],
        compiler_params=pltpu.CompilerParams(vmem_limit_bytes=VMEM_LIMIT),
        name="spread_uppers",
    )(packed, *after, *held)


def touch_kernel(panel, *refs):
    out = refs[-1]
    out[...] = panel[0:ID_ROWS, :]


def touched(panel, after=()):
    return pl.pallas_call(
        touch_kernel,
        out_shape=jax.ShapeDtypeStruct((ID_ROWS, panel.shape[1]), panel.dtype),
        in_specs=[whole_vmem()] + [pl.BlockSpec(memory_space=pl.ANY)] * len(after),
        out_specs=whole_vmem(),
        compiler_params=pltpu.CompilerParams(vmem_limit_bytes=VMEM_LIMIT),
        cost_estimate=pl.CostEstimate(flops=DECLARED_FLOPS, bytes_accessed=0, transcendentals=0),
        name="touch_chunk",
    )(panel, *after)


def place_group(parts, ids, first, slots, left, base):
    width = parts[0].shape[1]
    tiles = [(part, row) for part in parts for row in range(part.shape[0] // width)]
    ids = read_ids(ids[ids.shape[0] - ID_ROWS :, :])
    for tile, (part, row) in enumerate(tiles, first):
        at = pl.multiple_of(ids[tile, 0] * width, width)
        columns = pl.ds(pl.multiple_of(base + (tile // slots - first // slots) * width, width), width)
        left[pl.ds(at, width), columns] = part[row * width : (row + 1) * width, :]


def deep_of(plan, groups):
    slots, supernodes = plan
    return [supernodes - first // slots for _, _, first, _ in groups]


def place_groups(plan, groups, panels, uppers, left, right):
    slots, supernodes = plan
    width = panels[0][0].shape[1]
    column = lax.axis_index("col")
    layer = lax.axis_index("gz")
    deep = deep_of(plan, groups)
    left[...] = jnp.zeros_like(left)
    for side, (tiles, upper) in enumerate(zip(panels, uppers)):
        start = (layer if side == 0 else 1 - layer) * (sum(deep) * width) if len(panels) == 2 else 0
        for (members, ids, first, mask), span in zip(groups, deep):
            start = pl.multiple_of(start, width)
            rows = pl.multiple_of(((column ^ mask) * supernodes + first // slots) * width, width)
            right[pl.ds(start, span * width), :] = upper[pl.ds(rows, span * width), :]
            place_group([tiles[member] for member in members], tiles[ids], first, slots, left, start)
            start += span * width


def blocks_of(rows):
    size = rows // ROW_STEPS
    return [slice(i * size, (i + 1) * size) for i in range(ROW_STEPS)]


def product(left, right, block):
    width = left.shape[0] % (block.stop - block.start)
    return jnp.dot(
        left[width + block.start : width + block.stop, :], right[...], preferred_element_type=jnp.float32
    )


def sum_kernel(plan, groups, sides, bases, *refs):
    count = (len(refs) - sides - bases - 3) // sides
    panels = [refs[side * count : (side + 1) * count] for side in range(sides)]
    uppers = refs[sides * count : sides * count + sides]
    base_refs, (out, left, right) = refs[sides * (count + 1) : -3], refs[-3:]
    place_groups(plan, groups, panels, uppers, left, right)
    for block in blocks_of(out.shape[0]):
        update = product(left, right, block)
        if bases:
            update = base_refs[0][block, :] + update
        out[block, :] = update


def sum_groups(plan, groups, panels, uppers, shape, bases=()):
    sides = len(panels)
    width = panels[0][0].shape[1]
    depth = sides * sum(deep_of(plan, groups)) * width
    return pl.pallas_call(
        functools.partial(sum_kernel, plan, groups, sides, len(bases)),
        out_shape=jax.ShapeDtypeStruct(shape, jnp.float32),
        in_specs=[whole_vmem()] * (sides * (len(panels[0]) + 1) + len(bases)),
        out_specs=whole_vmem(),
        scratch_shapes=[
            pltpu.VMEM((shape[0] + width, depth), jnp.bfloat16),
            pltpu.VMEM((depth, shape[1]), jnp.bfloat16),
        ],
        compiler_params=pltpu.CompilerParams(vmem_limit_bytes=VMEM_LIMIT),
        cost_estimate=pl.CostEstimate(flops=SUM_FLOPS, bytes_accessed=0, transcendentals=0),
        name="sum_groups",
    )(*(panel for side in panels for panel in side), *uppers, *bases)


def finish_kernel(plan, groups, count, ancestor, early, *refs):
    panels = (refs[:count], refs[count : 2 * count])
    uppers, (out, left, right, result, sent) = refs[2 * count : 2 * count + 2], refs[-5:]
    place_groups(plan, groups, panels, uppers, left, right)
    copies = []
    for i, block in enumerate(blocks_of(out.shape[0])):
        result[block, :] = ancestor[block, :] - (early[block, :] + product(left, right, block))
        copy = pltpu.make_async_copy(result.at[block], out.at[block], sent.at[i])
        copy.start()
        copies.append(copy)
    for copy in copies:
        copy.wait()


def finish(plan, ancestor, early, groups, own, other, uppers, after):
    width = own[0].shape[1]
    depth = 2 * sum(deep_of(plan, groups)) * width
    return pl.pallas_call(
        functools.partial(finish_kernel, plan, groups, len(own)),
        out_shape=jax.ShapeDtypeStruct(ancestor.shape, jnp.float32),
        in_specs=[whole_vmem()] * (2 * len(own) + 4) + [pl.BlockSpec(memory_space=pl.ANY)] * len(after),
        out_specs=pl.BlockSpec(memory_space=pltpu.HBM),
        scratch_shapes=[
            pltpu.VMEM((ancestor.shape[0] + width, depth), jnp.bfloat16),
            pltpu.VMEM((depth, ancestor.shape[1]), jnp.bfloat16),
            pltpu.VMEM(ancestor.shape, jnp.float32),
            pltpu.SemaphoreType.DMA((ROW_STEPS,)),
        ],
        compiler_params=pltpu.CompilerParams(vmem_limit_bytes=VMEM_LIMIT),
        name="last_chunk_and_write",
    )(ancestor, early, *own, *other, *uppers, *after)


def swap(array, axis, mask):
    return lax.ppermute(array, axis, [(i, i ^ mask) for i in range(4)])


def siblings(array):
    return lax.ppermute(array, "gz", [(0, 1), (1, 0)])


def on_line_of_four(
    ancestor, lower_panel, row_ids, row_counts, diag_inverse, upper_panel, col_ids, col_counts
):
    supernodes, slots = lower_panel.shape[1:3]
    plan = (slots, supernodes)
    cut = 2 * supernodes * slots // 3
    both, first, second, packed = prepare(
        lower_panel,
        row_ids,
        row_counts,
        diag_inverse,
        upper_panel,
        col_ids,
        col_counts,
        cut,
    )
    near = swap(both, "col", 1)
    far_first = swap(first, "col", 2)
    far_second = swap(second, "col", 2)
    packed = lax.all_gather(packed, "row", axis=0, tiled=True)
    far_first, packed = lax.optimization_barrier((far_first, packed))
    last_first = swap(far_first, "col", 1)
    far_second, far_mark = lax.optimization_barrier((far_second, touched(far_second, [near])))
    last_second = swap(far_second, "col", 1)
    other_both, other_first = siblings(both), siblings(far_first)
    upper = spread_uppers(
        packed,
        [near, far_second, other_both],
        [ancestor],
        upper_panel.shape[2],
        supernodes,
        ancestor.shape[1],
    )
    uppers = (upper, siblings(upper))
    groups = (((0,), 0, 0, 0), ((1, 2), 1, 0, 2))
    early = sum_groups(plan, groups, [[both, far_first, far_second]], [upper], ancestor.shape)
    others = [other_both, other_first, siblings(far_second)]
    early = sum_groups(plan, groups, [others], [uppers[1]], ancestor.shape, [early])
    early = sum_groups(
        plan, (((0,), 0, 0, 1),), [[near], [siblings(near)]], uppers, ancestor.shape, [early]
    )
    last_first, first_mark = lax.optimization_barrier((last_first, touched(last_first)))
    last_second, second_mark = lax.optimization_barrier((last_second, touched(last_second, [early])))
    other_last = siblings(last_first)
    early = sum_groups(
        plan, (((0,), 0, 0, 3),), [[last_first], [other_last]], uppers, ancestor.shape, [early]
    )
    return finish(
        plan,
        ancestor,
        early,
        (((0,), 1, cut, 3),),
        [last_second, last_first],
        [siblings(last_second), other_last],
        uppers,
        [far_mark, first_mark, second_mark],
    )


def spread_tiles(tiles, ids, counts, blocks, rule):
    slot_index = jnp.arange(ids.shape[1], dtype=jnp.int32)
    alive = slot_index[None, :] < counts
    target = jnp.arange(blocks, dtype=jnp.int32)
    select = ((ids[:, :, None] == target[None, None, :]) & alive[:, :, None]).astype(jnp.bfloat16)
    return jnp.einsum(rule, select, tiles, preferred_element_type=jnp.float32).astype(jnp.bfloat16)


def on_device(
    ancestor, lower_panel, row_ids, row_counts, diag_inverse, upper_panel, col_ids, col_counts
):
    width = lower_panel.shape[-1]
    rows, columns = ancestor.shape
    solved = jnp.einsum(
        "ksab,kbc->ksac", lower_panel[0], diag_inverse[0], preferred_element_type=jnp.float32
    ).astype(jnp.bfloat16)
    piece = lax.all_gather((upper_panel[0], col_ids[0], col_counts[0]), "row", axis=0, tiled=True)
    upper_dense = spread_tiles(*piece, columns // width, "kcm,kcab->kamb").reshape(-1, columns)
    piece = lax.all_gather((solved, row_ids[0], row_counts[0]), "col", axis=0, tiled=True)
    lower_dense = spread_tiles(*piece, rows // width, "krl,krab->lakb").reshape(rows, -1)
    partial_sum = jnp.dot(lower_dense, upper_dense, preferred_element_type=jnp.float32)
    return ancestor - lax.psum(partial_sum, "gz")


def solution(mesh):
    placed = (
        P("row", "col"),
        P("gz", "col", "row", None, None),
        P("gz", "col", "row"),
        P("gz", "col", "row"),
        P("gz", "col", None, None),
        P("gz", "row", "col", None, None),
        P("gz", "row", "col"),
        P("gz", "row", "col"),
    )
    sizes = dict(mesh.shape)
    small = sizes["gz"] == 2 and sizes["row"] == 4 and sizes["col"] == 4

    def run(ancestor, lower_panel, *rest):
        two = lower_panel.shape[1] == 2 * sizes["col"]
        body = on_line_of_four if small and two else on_device
        return jax.shard_map(
            body, mesh=mesh, in_specs=placed, out_specs=P("row", "col"), check_vma=False
        )(ancestor, lower_panel, *rest)

    return run
```

```python
import functools

import jax
import jax.numpy as jnp
from jax import lax
from jax.experimental import pallas as pl
from jax.experimental.pallas import tpu as pltpu
from jax.sharding import PartitionSpec as P

VMEM_LIMIT = 24 * 1024 * 1024
ID_ROWS = 16
ROW_STEPS = 4
DECLARED_FLOPS = 10_000_000_000
SUM_FLOPS = 1_000_000_000


def whole_vmem():
    return pl.BlockSpec(memory_space=pltpu.VMEM)


def pack_ids(ids, counts, supernodes, slots, width):
    at_row = lax.broadcasted_iota(jnp.int32, (ID_ROWS, width), 0)
    rows = jnp.zeros((ID_ROWS, width), jnp.int32)
    for k in range(supernodes):
        for s in range(slots):
            value = jnp.where(s < counts[0, 0, k], ids[0, k, s] + 1, 0)
            rows = jnp.where(at_row == k * slots + s, value, rows)
    return rows.astype(jnp.float32).astype(jnp.bfloat16)


def read_ids(rows):
    return rows.astype(jnp.float32).astype(jnp.int32)


def prepare_kernel(
    row_ids_in, row_counts_in, col_ids_in, col_counts_in, lower_in, inverse_in, upper_in,
    both, first, second, packed,
    row_ids, row_counts, col_ids, col_counts, lower, inverse, upper, arrived,
):
    supernodes, slots, width, _ = lower.shape
    tall = slots * width
    cut = first.shape[0] - ID_ROWS
    pairs = (
        (row_ids_in, row_ids),
        (row_counts_in, row_counts),
        (inverse_in.at[0], inverse),
        (lower_in.at[0, 0], lower.at[0]),
        (lower_in.at[0, 1], lower.at[1]),
        (col_ids_in, col_ids),
        (col_counts_in, col_counts),
        (upper_in.at[0], upper),
    )
    copies = [pltpu.make_async_copy(src, dst, arrived.at[n]) for n, (src, dst) in enumerate(pairs)]
    for copy in copies:
        copy.start()
    for copy in copies[:3]:
        copy.wait()
    ids = pack_ids(row_ids, row_counts, supernodes, slots, width)
    first[cut:, :] = ids
    both[supernodes * tall :, :] = ids
    for k in range(supernodes):
        copies[3 + k].wait()
        solved = jnp.dot(lower[k].reshape(tall, width), inverse[k], preferred_element_type=jnp.float32)
        solved = solved.astype(jnp.bfloat16)
        start, stop = k * tall, (k + 1) * tall
        both[start:stop, :] = solved
        middle = min(max(cut, start), stop)
        if middle > start:
            first[start:middle, :] = solved[: middle - start]
        if middle < stop:
            second[middle - cut : stop - cut, :] = solved[middle - start :]
    for copy in copies[5:]:
        copy.wait()
    slots = upper.shape[1]
    tall = slots * width
    for k in range(supernodes):
        packed[k * tall : (k + 1) * tall, :] = upper[k].reshape(tall, width)
    packed[supernodes * tall :, :] = pack_ids(col_ids, col_counts, supernodes, slots, width)


def prepare(lower, row_ids, row_counts, inverse, upper, col_ids, col_counts, cut):
    _, supernodes, slots, width, _ = lower.shape
    tiles = supernodes * slots
    row_counts = jnp.swapaxes(row_counts, 1, 2)
    col_counts = jnp.swapaxes(col_counts, 1, 2)
    return pl.pallas_call(
        prepare_kernel,
        out_shape=(
            jax.ShapeDtypeStruct((tiles * width + ID_ROWS, width), jnp.bfloat16),
            jax.ShapeDtypeStruct((cut * width + ID_ROWS, width), jnp.bfloat16),
            jax.ShapeDtypeStruct(((tiles - cut) * width, width), jnp.bfloat16),
            jax.ShapeDtypeStruct((supernodes * upper.shape[2] * width + ID_ROWS, width), jnp.bfloat16),
        ),
        in_specs=[pl.BlockSpec(memory_space=pltpu.HBM)] * 7,
        out_specs=(whole_vmem(),) * 4,
        scratch_shapes=[
            pltpu.SMEM(row_ids.shape, jnp.int32),
            pltpu.SMEM(row_counts.shape, jnp.int32),
            pltpu.SMEM(col_ids.shape, jnp.int32),
            pltpu.SMEM(col_counts.shape, jnp.int32),
            pltpu.VMEM(lower.shape[1:], jnp.bfloat16),
            pltpu.VMEM(inverse.shape[1:], jnp.bfloat16),
            pltpu.VMEM(upper.shape[1:], jnp.bfloat16),
            pltpu.SemaphoreType.DMA((8,)),
        ],
        compiler_params=pltpu.CompilerParams(vmem_limit_bytes=VMEM_LIMIT),
        name="solve_and_pack",
    )(
        *(
            pltpu.with_memory_space_constraint(array, pltpu.HBM)
            for array in (row_ids, row_counts, col_ids, col_counts, lower, inverse, upper)
        )
    )


def spread_kernel(slots, supernodes, packed, *refs):
    out, padded = refs[-2:]
    width = packed.shape[1]
    piece = supernodes * slots * width + ID_ROWS
    padded[...] = jnp.zeros_like(padded)
    for group in range(packed.shape[0] // piece):
        start = group * piece
        ids = read_ids(packed[start + piece - ID_ROWS : start + piece, :])
        for k in range(supernodes):
            rows = slice((group * supernodes + k) * width, (group * supernodes + k + 1) * width)
            for s in range(slots):
                tile = k * slots + s
                at = pl.multiple_of(ids[tile, 0] * width, width)
                padded[rows, pl.ds(at, width)] = packed[start + tile * width : start + (tile + 1) * width, :]
    out[...] = padded[:, width:]


def spread_uppers(packed, after, held, slots, supernodes, columns):
    width = packed.shape[1]
    deep = packed.shape[0] // (supernodes * slots * width + ID_ROWS) * supernodes * width
    return pl.pallas_call(
        functools.partial(spread_kernel, slots, supernodes),
        out_shape=jax.ShapeDtypeStruct((deep, columns), jnp.bfloat16),
        in_specs=[whole_vmem()]
        + [pl.BlockSpec(memory_space=pl.ANY)] * len(after)
        + [whole_vmem()] * len(held),
        out_specs=whole_vmem(),
        scratch_shapes=[pltpu.VMEM((deep, columns + width), jnp.bfloat16)],
        compiler_params=pltpu.CompilerParams(vmem_limit_bytes=VMEM_LIMIT),
        name="spread_uppers",
    )(packed, *after, *held)


def touch_kernel(panel, *refs):
    out = refs[-1]
    out[...] = panel[0:ID_ROWS, :]


def touched(panel, after=()):
    return pl.pallas_call(
        touch_kernel,
        out_shape=jax.ShapeDtypeStruct((ID_ROWS, panel.shape[1]), panel.dtype),
        in_specs=[whole_vmem()] + [pl.BlockSpec(memory_space=pl.ANY)] * len(after),
        out_specs=whole_vmem(),
        compiler_params=pltpu.CompilerParams(vmem_limit_bytes=VMEM_LIMIT),
        cost_estimate=pl.CostEstimate(flops=DECLARED_FLOPS, bytes_accessed=0, transcendentals=0),
        name="touch_chunk",
    )(panel, *after)


def place_group(parts, ids, first, slots, left, base):
    width = parts[0].shape[1]
    tiles = [(part, row) for part in parts for row in range(part.shape[0] // width)]
    ids = read_ids(ids[ids.shape[0] - ID_ROWS :, :])
    for tile, (part, row) in enumerate(tiles, first):
        at = pl.multiple_of(ids[tile, 0] * width, width)
        columns = pl.ds(pl.multiple_of(base + (tile // slots - first // slots) * width, width), width)
        left[pl.ds(at, width), columns] = part[row * width : (row + 1) * width, :]


def deep_of(plan, groups):
    slots, supernodes = plan
    return [supernodes - first // slots for _, _, first, _ in groups]


def place_groups(plan, groups, panels, uppers, left, right):
    slots, supernodes = plan
    width = panels[0][0].shape[1]
    column = lax.axis_index("col")
    layer = lax.axis_index("gz")
    deep = deep_of(plan, groups)
    left[...] = jnp.zeros_like(left)
    for side, (tiles, upper) in enumerate(zip(panels, uppers)):
        start = (layer if side == 0 else 1 - layer) * (sum(deep) * width) if len(panels) == 2 else 0
        for (members, ids, first, mask), span in zip(groups, deep):
            start = pl.multiple_of(start, width)
            rows = pl.multiple_of(((column ^ mask) * supernodes + first // slots) * width, width)
            right[pl.ds(start, span * width), :] = upper[pl.ds(rows, span * width), :]
            place_group([tiles[member] for member in members], tiles[ids], first, slots, left, start)
            start += span * width


def blocks_of(rows):
    size = rows // ROW_STEPS
    return [slice(i * size, (i + 1) * size) for i in range(ROW_STEPS)]


def product(left, right, block):
    width = left.shape[0] % (block.stop - block.start)
    return jnp.dot(
        left[width + block.start : width + block.stop, :], right[...], preferred_element_type=jnp.float32
    )


def sum_kernel(plan, groups, sides, bases, *refs):
    count = (len(refs) - sides - bases - 3) // sides
    panels = [refs[side * count : (side + 1) * count] for side in range(sides)]
    uppers = refs[sides * count : sides * count + sides]
    base_refs, (out, left, right) = refs[sides * (count + 1) : -3], refs[-3:]
    place_groups(plan, groups, panels, uppers, left, right)
    for block in blocks_of(out.shape[0]):
        update = product(left, right, block)
        if bases:
            update = base_refs[0][block, :] + update
        out[block, :] = base_refs[1][block, :] - update if bases == 2 else update


def sum_groups(plan, groups, panels, uppers, shape, bases=()):
    sides = len(panels)
    width = panels[0][0].shape[1]
    depth = sides * sum(deep_of(plan, groups)) * width
    return pl.pallas_call(
        functools.partial(sum_kernel, plan, groups, sides, len(bases)),
        out_shape=jax.ShapeDtypeStruct(shape, jnp.float32),
        in_specs=[whole_vmem()] * (sides * (len(panels[0]) + 1) + len(bases)),
        out_specs=whole_vmem(),
        scratch_shapes=[
            pltpu.VMEM((shape[0] + width, depth), jnp.bfloat16),
            pltpu.VMEM((depth, shape[1]), jnp.bfloat16),
        ],
        compiler_params=pltpu.CompilerParams(vmem_limit_bytes=VMEM_LIMIT),
        cost_estimate=pl.CostEstimate(flops=SUM_FLOPS, bytes_accessed=0, transcendentals=0),
        name="sum_groups",
    )(*(panel for side in panels for panel in side), *uppers, *bases)


def finish_kernel(plan, groups, count, base, *refs):
    panels = (refs[:count], refs[count : 2 * count])
    uppers, (out, left, right, result, sent) = refs[2 * count : 2 * count + 2], refs[-5:]
    place_groups(plan, groups, panels, uppers, left, right)
    copies = []
    for i, block in enumerate(blocks_of(out.shape[0])):
        result[block, :] = base[block, :] - product(left, right, block)
        copy = pltpu.make_async_copy(result.at[block], out.at[block], sent.at[i])
        copy.start()
        copies.append(copy)
    for copy in copies:
        copy.wait()


def finish(plan, base, groups, own, other, uppers, after):
    width = own[0].shape[1]
    depth = 2 * sum(deep_of(plan, groups)) * width
    return pl.pallas_call(
        functools.partial(finish_kernel, plan, groups, len(own)),
        out_shape=jax.ShapeDtypeStruct(base.shape, jnp.float32),
        in_specs=[whole_vmem()] * (2 * len(own) + 3) + [pl.BlockSpec(memory_space=pl.ANY)] * len(after),
        out_specs=pl.BlockSpec(memory_space=pltpu.HBM),
        scratch_shapes=[
            pltpu.VMEM((base.shape[0] + width, depth), jnp.bfloat16),
            pltpu.VMEM((depth, base.shape[1]), jnp.bfloat16),
            pltpu.VMEM(base.shape, jnp.float32),
            pltpu.SemaphoreType.DMA((ROW_STEPS,)),
        ],
        compiler_params=pltpu.CompilerParams(vmem_limit_bytes=VMEM_LIMIT),
        name="last_chunk_and_write",
    )(base, *own, *other, *uppers, *after)


def swap(array, axis, mask):
    return lax.ppermute(array, axis, [(i, i ^ mask) for i in range(4)])


def siblings(array):
    return lax.ppermute(array, "gz", [(0, 1), (1, 0)])


def on_line_of_four(
    ancestor, lower_panel, row_ids, row_counts, diag_inverse, upper_panel, col_ids, col_counts
):
    supernodes, slots = lower_panel.shape[1:3]
    plan = (slots, supernodes)
    cut = 2 * supernodes * slots // 3
    both, first, second, packed = prepare(
        lower_panel,
        row_ids,
        row_counts,
        diag_inverse,
        upper_panel,
        col_ids,
        col_counts,
        cut,
    )
    near = swap(both, "col", 1)
    far_first = swap(first, "col", 2)
    far_second = swap(second, "col", 2)
    packed = lax.all_gather(packed, "row", axis=0, tiled=True)
    far_first, packed = lax.optimization_barrier((far_first, packed))
    last_first = swap(far_first, "col", 1)
    far_second, far_mark = lax.optimization_barrier((far_second, touched(far_second, [near])))
    last_second = swap(far_second, "col", 1)
    other_both, other_first = siblings(both), siblings(far_first)
    upper = spread_uppers(
        packed,
        [near, far_second, other_both],
        [ancestor],
        upper_panel.shape[2],
        supernodes,
        ancestor.shape[1],
    )
    uppers = (upper, siblings(upper))
    groups = (((0,), 0, 0, 0), ((1, 2), 1, 0, 2))
    early = sum_groups(plan, groups, [[both, far_first, far_second]], [upper], ancestor.shape)
    others = [other_both, other_first, siblings(far_second)]
    early = sum_groups(plan, groups, [others], [uppers[1]], ancestor.shape, [early])
    early = sum_groups(
        plan, (((0,), 0, 0, 1),), [[near], [siblings(near)]], uppers, ancestor.shape, [early]
    )
    last_first, first_mark = lax.optimization_barrier((last_first, touched(last_first)))
    last_second, second_mark = lax.optimization_barrier((last_second, touched(last_second, [early])))
    other_last = siblings(last_first)
    base = sum_groups(
        plan, (((0,), 0, 0, 3),), [[last_first], [other_last]], uppers, ancestor.shape, [early, ancestor]
    )
    return finish(
        plan,
        base,
        (((0,), 1, cut, 3),),
        [last_second, last_first],
        [siblings(last_second), other_last],
        uppers,
        [far_mark, first_mark, second_mark],
    )


def spread_tiles(tiles, ids, counts, blocks, rule):
    slot_index = jnp.arange(ids.shape[1], dtype=jnp.int32)
    alive = slot_index[None, :] < counts
    target = jnp.arange(blocks, dtype=jnp.int32)
    select = ((ids[:, :, None] == target[None, None, :]) & alive[:, :, None]).astype(jnp.bfloat16)
    return jnp.einsum(rule, select, tiles, preferred_element_type=jnp.float32).astype(jnp.bfloat16)


def on_device(
    ancestor, lower_panel, row_ids, row_counts, diag_inverse, upper_panel, col_ids, col_counts
):
    width = lower_panel.shape[-1]
    rows, columns = ancestor.shape
    solved = jnp.einsum(
        "ksab,kbc->ksac", lower_panel[0], diag_inverse[0], preferred_element_type=jnp.float32
    ).astype(jnp.bfloat16)
    piece = lax.all_gather((upper_panel[0], col_ids[0], col_counts[0]), "row", axis=0, tiled=True)
    upper_dense = spread_tiles(*piece, columns // width, "kcm,kcab->kamb").reshape(-1, columns)
    piece = lax.all_gather((solved, row_ids[0], row_counts[0]), "col", axis=0, tiled=True)
    lower_dense = spread_tiles(*piece, rows // width, "krl,krab->lakb").reshape(rows, -1)
    partial_sum = jnp.dot(lower_dense, upper_dense, preferred_element_type=jnp.float32)
    return ancestor - lax.psum(partial_sum, "gz")


def solution(mesh):
    placed = (
        P("row", "col"),
        P("gz", "col", "row", None, None),
        P("gz", "col", "row"),
        P("gz", "col", "row"),
        P("gz", "col", None, None),
        P("gz", "row", "col", None, None),
        P("gz", "row", "col"),
        P("gz", "row", "col"),
    )
    sizes = dict(mesh.shape)
    small = sizes["gz"] == 2 and sizes["row"] == 4 and sizes["col"] == 4

    def run(ancestor, lower_panel, *rest):
        two = lower_panel.shape[1] == 2 * sizes["col"]
        body = on_line_of_four if small and two else on_device
        return jax.shard_map(
            body, mesh=mesh, in_specs=placed, out_specs=P("row", "col"), check_vma=False
        )(ancestor, lower_panel, *rest)

    return run
```
